32 devices in a mesh: dp: 4 (over z), seq: 8 (over y, x, core).
Axes of the slice: x: 2, y: 2, z: 4, core: 2. Of those that a mesh axis runs over, the one named last changes fastest.
Arguments:
- x_rows: bfloat16 [4, 1024, 1024], P('dp', 'seq'), may hold values from -6 to 6
- lengths: int32 [4, 8], P('dp'), may hold values from 1 to 512, 1024 in all within a row
- targets: int32 [4, 8], P('dp'), may hold values from 1 to 64
- w_in: bfloat16 [1024, 2048], replicated, may hold values from -0.1875 to 0.1875
- w_out: bfloat16 [512, 1024], replicated, may hold values from -0.25 to 0.25
- w_score: bfloat16 [1024, 256], replicated, may hold values from -0.1875 to 0.1875
- head_score: float32 [256], replicated, may hold values from -0.375 to 0.375
- grad_out: bfloat16 [4, 1024, 1024], P('dp', 'seq'), may hold values from -6 to 6
- grad_score: float32 [4, 1024], P('dp', 'seq'), may hold values from -6 to 6
Outputs:
- d_x: bfloat16 [4, 1024, 1024], P('dp', 'seq')
- d_w_in: float32 [1024, 2048], P('seq', 'dp')
- d_w_out: float32 [512, 1024], P('seq', 'dp')
- d_w_score: float32 [1024, 256], P('seq', 'dp')
- d_head: float32 [256], replicated
The draws below stay inside these ranges and needn't reach their ends.
Inputs may be any that keep to these rules, and one draw needn't show every extreme that they name: Each row lists the lengths of 8 histories packed end to end in the 1024 positions of a group; they sum to 1024 and the largest is 512.
All inputs are finite; a program needn't handle non-finite values.
Results may differ from the reference program's by a relative error of at most 0.0084.
Values may be sent and summed in bfloat16 or wider, within the bound.
A program may use at most 64 MiB of HBM per device.

```python
import math
import jax
import jax.numpy as jnp
import numpy as np
from jax import lax

D = 1024
HEADS = 4
DH = 128
DM = 256
HIST = 8
TGT = 64
TOKENS = 1024
MOST = 512
GROUPS = 4


def with_ends(values, rng, low, largest):
    longest = values.shape.index(max(values.shape))
    spots = []
    for shift in (0, 1):
        where = [jax.random.randint(jax.random.fold_in(rng, axis), (), 0, length) for axis, length in enumerate(values.shape)]
        where[longest] = (where[longest] + shift) % values.shape[longest]
        spots.append(tuple(where))
    return values.at[spots[0]].set(low).at[spots[1]].set(largest)


def levels(own_key, extent, shards, low, largest):
    def one(axis_at, blocks):
        steps = jax.random.uniform(jax.random.fold_in(jax.random.fold_in(own_key, 6), axis_at), (blocks,), jnp.float32, low / len(shards), largest / len(shards))
        return jnp.repeat(jnp.exp(steps), extent[axis_at] // blocks).reshape((-1,) + (1,) * (len(extent) - axis_at - 1))

    level = one(*shards[0])
    for cut in shards[1:]:
        level = level * one(*cut)
    return level


def profile(count, total, bound, skew):
    weights = [(1 << 20) // math.isqrt(rank ** skew) + 1 for rank in range(2, count + 1)]
    spare, given = total - bound - (count - 1), [1] * (count - 1)
    while spare > 0:
        candidates = [i for i in range(count - 1) if given[i] < bound]
        pool, budget = sum([weights[i] for i in candidates]), spare
        for i in candidates:
            addition = min(bound - given[i], max(1, budget * weights[i] // pool), spare)
            given[i] = given[i] + addition
            spare = spare - addition
    return np.array([bound] + given)


def ragged(own_key, count, total, limit, skew):
    if count == 2:
        one = jax.random.randint(own_key, (), max(1, total - limit), min(limit, total - 1) + 1)
        return jnp.stack([one, total - one])
    tallies = jnp.asarray(profile(count, total, limit, skew), jnp.int32)
    couples = (count - 1) // 2
    giver, sink = tallies[1:1 + 2 * couples:2], tallies[2:2 + 2 * couples:2]
    slack = jnp.minimum(giver - 1, limit - sink)
    moved = jax.random.randint(jax.random.fold_in(own_key, 1), (couples,), 0, 1 << 20) % (slack + 1)
    tallies = tallies.at[1:1 + 2 * couples:2].set(giver - moved).at[2:2 + 2 * couples:2].set(sink + moved)
    return tallies[jax.random.permutation(jax.random.fold_in(own_key, 2), count)]


def normal_values(rng, shape, scale, most, shards=(), kind=jnp.bfloat16):
    values = jax.random.normal(rng, shape, jnp.float32) * scale
    if len(shards) > 0:
        values = levels(rng, shape, shards, -0.22, 0.18) * values
    return jnp.clip(values, min=-most, max=most).astype(kind)


def setup_inputs(seed: int = 0) -> dict:
    arg_keys = jax.random.split(jax.random.key(seed), 10)
    return {
        "x_rows": normal_values(arg_keys[0], (GROUPS, TOKENS, D), 1.0, 6.0, ((0, 4), (1, 8))),
        "lengths": jax.vmap(lambda own: ragged(own, HIST, TOKENS, MOST, 2))(jax.random.split(arg_keys[1], GROUPS)).reshape((GROUPS, HIST)).astype(jnp.int32),
        "targets": with_ends(jax.random.randint(arg_keys[2], (GROUPS, HIST), 1, TGT + 1), jax.random.fold_in(arg_keys[2], 1), 1, TGT).astype(jnp.int32),
        "w_in": normal_values(arg_keys[3], (D, 4 * HEADS * DH), D ** -0.5, 0.1875),
        "w_out": normal_values(arg_keys[4], (HEADS * DH, D), (HEADS * DH) ** -0.5, 0.25),
        "w_score": normal_values(arg_keys[5], (D, DM), D ** -0.5, 0.1875),
        "head_score": normal_values(arg_keys[6], (DM,), DM ** -0.5, 0.375, (), jnp.float32),
        "grad_out": normal_values(arg_keys[7], (GROUPS, TOKENS, D), 1.0, 6.0, ((0, 4), (1, 8))),
        "grad_score": normal_values(arg_keys[8], (GROUPS, TOKENS), 1.0, 6.0, ((0, 4), (1, 8)), jnp.float32),
    }


NORM_EPS = 1e-05

def silu_slope(value):
    sigma = jax.nn.sigmoid(value)
    return sigma * (1.0 + value * (1.0 - sigma))

def norm_rows(value):
    centre = value - lax.optimization_barrier(jnp.mean(value, axis=-1, keepdims=True))
    inverse = lax.rsqrt(lax.optimization_barrier(jnp.mean(centre * centre, axis=-1, keepdims=True)) + NORM_EPS)
    return (centre * inverse, inverse)

def norm_back(grad, normed, inverse):
    return inverse * (grad - lax.optimization_barrier(jnp.mean(grad, axis=-1, keepdims=True)) - normed * lax.optimization_barrier(jnp.mean(grad * normed, axis=-1, keepdims=True)))

def row_marks(positions, lengths, targets):
    ends = jnp.cumsum(lengths).astype(jnp.int32)
    starts = ends - lengths
    counts = jnp.minimum(targets, lengths - 1)
    inside = (positions[:, None] >= starts[None, :]) & (positions[:, None] < ends[None, :])
    segment = lax.optimization_barrier(jnp.sum((positions[:, None] >= ends[None, :]).astype(jnp.int32), axis=1))
    first_target = lax.optimization_barrier(jnp.sum(jnp.where(inside, (ends - counts)[None, :], 0), axis=1))
    return (segment, positions >= first_target)

def visible(query_pos, query_seg, key_pos, key_seg, key_tgt):
    same_hist = query_seg[:, None] == key_seg[None, :]
    causal = key_pos[None, :] <= query_pos[:, None]
    open_key = jnp.logical_not(key_tgt)[None, :] | (key_pos[None, :] == query_pos[:, None])
    return (same_hist & causal & open_key)[None, :, :]

def weights_of(query_b, key_b, mask, divisor):
    raw_scores = jnp.einsum('rhd,chd->hrc', query_b.astype(jnp.float32), key_b.astype(jnp.float32)) * DH ** (-0.5)
    attn_b = jnp.where(mask, jax.nn.silu(raw_scores) / divisor, 0.0).astype(jnp.bfloat16)
    return (raw_scores, attn_b)

def score_grads(raw_scores, mask, grad_b, value_b, divisor):
    grad_attn = jnp.einsum('rhd,chd->hrc', grad_b.astype(jnp.float32), value_b.astype(jnp.float32))
    factor = jnp.where(mask, silu_slope(raw_scores) * DH ** (-0.5) / divisor, 0.0)
    return (grad_attn * factor).astype(jnp.bfloat16)

def group_grads(x_rows, lengths, targets, grad_out, grad_score, w_in, w_out, w_score, head_score):
    width = HEADS * DH
    positions = jnp.arange(TOKENS, dtype=jnp.int32)
    segment, target = row_marks(positions, lengths, targets)
    divisor = float(TOKENS // 2)
    x_float = x_rows.astype(jnp.float32)
    normed, inverse = norm_rows(x_float)
    normed_b = normed.astype(jnp.bfloat16)
    pre_act = jnp.dot(normed_b, w_in, preferred_element_type=jnp.float32)
    hidden_b = jax.nn.silu(pre_act).astype(jnp.bfloat16)
    gate_b = hidden_b[:, 0:width]
    value_b = hidden_b[:, width:2 * width].reshape(TOKENS, HEADS, DH)
    query_b = hidden_b[:, 2 * width:3 * width].reshape(TOKENS, HEADS, DH)
    key_b = hidden_b[:, 3 * width:4 * width].reshape(TOKENS, HEADS, DH)
    block_rows = math.gcd(512, TOKENS)
    block_count = TOKENS // block_rows

    def query_slice(array, number):
        return lax.dynamic_slice_in_dim(array, number * block_rows, block_rows, 0)

    def forward_block(number):
        block_pos = query_slice(positions, number)
        mask = visible(block_pos, query_slice(segment, number), positions, segment, target)
        raw_scores, attn_b = weights_of(query_slice(query_b, number), key_b, mask, divisor)
        return jnp.einsum('hrc,chd->rhd', attn_b.astype(jnp.float32), value_b.astype(jnp.float32))
    attended = lax.map(forward_block, jnp.arange(block_count, dtype=jnp.int32)).reshape(TOKENS, width)
    onorm, att_inverse = norm_rows(attended)
    gate_f = gate_b.astype(jnp.float32)
    gated_b = (onorm * gate_f).astype(jnp.bfloat16)
    output = x_float + jnp.dot(gated_b, w_out, preferred_element_type=jnp.float32)
    out_b = output.astype(jnp.bfloat16)
    mid_act = jnp.dot(out_b, w_score, preferred_element_type=jnp.float32)
    weight_c = grad_score * target.astype(jnp.float32)
    head_part = lax.optimization_barrier(jnp.sum(weight_c[:, None] * jax.nn.silu(mid_act), axis=0))
    d_mid_b = (weight_c[:, None] * head_score[None, :] * silu_slope(mid_act)).astype(jnp.bfloat16)
    score_part = jnp.dot(out_b.T, d_mid_b, preferred_element_type=jnp.float32)
    d_total = grad_out.astype(jnp.float32) + jnp.dot(d_mid_b, w_score.T, preferred_element_type=jnp.float32)
    d_total_b = d_total.astype(jnp.bfloat16)
    out_part = jnp.dot(gated_b.T, d_total_b, preferred_element_type=jnp.float32)
    d_gated = jnp.dot(d_total_b, w_out.T, preferred_element_type=jnp.float32)
    d_gate = d_gated * onorm
    d_att_b = norm_back(d_gated * gate_f, onorm, att_inverse).astype(jnp.bfloat16).reshape(TOKENS, HEADS, DH)

    def query_grad_block(number):
        block_pos = query_slice(positions, number)
        mask = visible(block_pos, query_slice(segment, number), positions, segment, target)
        raw_scores, attn_b = weights_of(query_slice(query_b, number), key_b, mask, divisor)
        d_raw_b = score_grads(raw_scores, mask, query_slice(d_att_b, number), value_b, divisor)
        return jnp.einsum('hrc,chd->rhd', d_raw_b.astype(jnp.float32), key_b.astype(jnp.float32))

    def key_grad_block(number):
        key_pos = query_slice(positions, number)
        mask = visible(positions, segment, key_pos, query_slice(segment, number), query_slice(target, number))
        key_blk = query_slice(key_b, number)
        value_blk = query_slice(value_b, number)
        raw_scores, attn_b = weights_of(query_b, key_blk, mask, divisor)
        d_raw_b = score_grads(raw_scores, mask, d_att_b, value_blk, divisor)
        d_key = jnp.einsum('hrc,rhd->chd', d_raw_b.astype(jnp.float32), query_b.astype(jnp.float32))
        d_value = jnp.einsum('hrc,rhd->chd', attn_b.astype(jnp.float32), d_att_b.astype(jnp.float32))
        return (d_key, d_value)
    d_query = lax.map(query_grad_block, jnp.arange(block_count, dtype=jnp.int32)).reshape(TOKENS, width)
    d_key, d_value = lax.map(key_grad_block, jnp.arange(block_count, dtype=jnp.int32))
    d_hidden = jnp.concatenate([d_gate, d_value.reshape(TOKENS, width), d_query, d_key.reshape(TOKENS, width)], axis=1)
    d_pre_b = (d_hidden * silu_slope(pre_act)).astype(jnp.bfloat16)
    in_part = jnp.dot(normed_b.T, d_pre_b, preferred_element_type=jnp.float32)
    d_normed = jnp.dot(d_pre_b, w_in.T, preferred_element_type=jnp.float32)
    d_x = (d_total + norm_back(d_normed, normed, inverse)).astype(jnp.bfloat16)
    return (d_x, in_part, out_part, score_part, head_part)

def reference(x_rows, lengths, targets, w_in, w_out, w_score, head_score, grad_out, grad_score):

    def one_group(items):
        return group_grads(items[0], items[1], items[2], items[3], items[4], w_in, w_out, w_score, head_score)
    d_x, in_parts, out_parts, score_parts, head_parts = lax.map(one_group, (x_rows, lengths, targets, grad_out, grad_score))
    return (d_x, lax.optimization_barrier(jnp.sum(in_parts, axis=0)), lax.optimization_barrier(jnp.sum(out_parts, axis=0)), lax.optimization_barrier(jnp.sum(score_parts, axis=0)), lax.optimization_barrier(jnp.sum(head_parts, axis=0)))
```

```python
import jax
import jax.numpy as jnp
from jax import lax
from jax.sharding import PartitionSpec as P

HEADS = 4
DH = 128


NORM_EPS = 1e-05


def silu_slope(value):
    sigma = jax.nn.sigmoid(value)
    return sigma * (1.0 + value * (1.0 - sigma))


def norm_rows(value):
    centre = value - jnp.mean(value, axis=-1, keepdims=True)
    inverse = lax.rsqrt(jnp.mean(centre * centre, axis=-1, keepdims=True) + NORM_EPS)
    return (centre * inverse, inverse)


def norm_back(grad, normed, inverse):
    return inverse * (
        grad
        - jnp.mean(grad, axis=-1, keepdims=True)
        - normed * jnp.mean(grad * normed, axis=-1, keepdims=True)
    )


def row_marks(positions, lengths, targets):
    ends = jnp.cumsum(lengths)
    starts = ends - lengths
    counts = jnp.minimum(targets, lengths - 1)
    inside = (positions[:, None] >= starts[None, :]) & (positions[:, None] < ends[None, :])
    segment = jnp.sum((positions[:, None] >= ends[None, :]).astype(jnp.int32), axis=1)
    first_target = jnp.sum(jnp.where(inside, (ends - counts)[None, :], 0), axis=1)
    return (segment, positions >= first_target)


def visible(query_pos, query_seg, key_pos, key_seg, key_tgt):
    same_hist = query_seg[:, None] == key_seg[None, :]
    causal = key_pos[None, :] <= query_pos[:, None]
    open_key = jnp.logical_not(key_tgt)[None, :] | (key_pos[None, :] == query_pos[:, None])
    return (same_hist & causal & open_key)[None, :, :]


def weights_of(query_b, key_b, mask, divisor):
    raw_scores = jnp.einsum(
        "rhd,chd->hrc", query_b, key_b, preferred_element_type=jnp.float32
    ) * DH ** (-0.5)
    attn_b = jnp.where(mask, jax.nn.silu(raw_scores) / divisor, 0.0).astype(jnp.bfloat16)
    return (raw_scores, attn_b)


def score_grads(raw_scores, mask, grad_b, value_b, divisor):
    grad_attn = jnp.einsum("rhd,chd->hrc", grad_b, value_b, preferred_element_type=jnp.float32)
    factor = jnp.where(mask, silu_slope(raw_scores) * DH ** (-0.5) / divisor, 0.0)
    return (grad_attn * factor).astype(jnp.bfloat16)


def on_device(x_rows, lengths, targets, w_in, w_out, w_score, head_score, grad_out, grad_score):
    rows = x_rows.shape[1]
    seq_count = lax.axis_size("seq")
    total = rows * seq_count
    width = w_out.shape[0]
    divisor = float(total // 2)
    hist_len = lengths[0]
    hist_tgt = targets[0]
    own_start = lax.axis_index("seq") * rows
    positions = own_start + jnp.arange(rows, dtype=jnp.int32)
    all_pos = jnp.arange(total, dtype=jnp.int32)
    segment, target = row_marks(positions, hist_len, hist_tgt)
    all_seg, all_tgt = row_marks(all_pos, hist_len, hist_tgt)
    x_float = x_rows[0].astype(jnp.float32)
    normed, inverse = norm_rows(x_float)
    normed_b = normed.astype(jnp.bfloat16)
    pre_act = jnp.dot(normed_b, w_in, preferred_element_type=jnp.float32)
    hidden_b = jax.nn.silu(pre_act).astype(jnp.bfloat16)
    gate_b = hidden_b[:, 0:width]
    value_b = hidden_b[:, width : 2 * width].reshape(rows, HEADS, DH)
    query_b = hidden_b[:, 2 * width : 3 * width].reshape(rows, HEADS, DH)
    key_b = hidden_b[:, 3 * width : 4 * width].reshape(rows, HEADS, DH)
    moved = lax.all_gather(hidden_b[:, width:], "seq", axis=0, tiled=True)
    value_all, query_all, key_all = (
        moved[:, at * width : (at + 1) * width].reshape(total, HEADS, DH) for at in range(3)
    )
    mask = visible(positions, segment, all_pos, all_seg, all_tgt)
    raw_scores, attn_b = weights_of(query_b, key_all, mask, divisor)
    attended = jnp.einsum("hrc,chd->rhd", attn_b, value_all, preferred_element_type=jnp.float32)
    attended = attended.reshape(rows, width)
    onorm, att_inverse = norm_rows(attended)
    gate_f = gate_b.astype(jnp.float32)
    gated_b = (onorm * gate_f).astype(jnp.bfloat16)
    output = x_float + jnp.dot(gated_b, w_out, preferred_element_type=jnp.float32)
    out_b = output.astype(jnp.bfloat16)
    mid_act = jnp.dot(out_b, w_score, preferred_element_type=jnp.float32)
    weight_c = grad_score[0] * target.astype(jnp.float32)
    head_part = jnp.sum(weight_c[:, None] * jax.nn.silu(mid_act), axis=0)
    d_mid_b = (weight_c[:, None] * head_score[None, :] * silu_slope(mid_act)).astype(jnp.bfloat16)
    score_part = jnp.dot(out_b.T, d_mid_b, preferred_element_type=jnp.float32)
    d_total = grad_out[0].astype(jnp.float32) + jnp.dot(
        d_mid_b, w_score.T, preferred_element_type=jnp.float32
    )
    d_total_b = d_total.astype(jnp.bfloat16)
    out_part = jnp.dot(gated_b.T, d_total_b, preferred_element_type=jnp.float32)
    d_gated = jnp.dot(d_total_b, w_out.T, preferred_element_type=jnp.float32)
    d_gate = d_gated * onorm
    d_att_b = (
        norm_back(d_gated * gate_f, onorm, att_inverse)
        .astype(jnp.bfloat16)
        .reshape(rows, HEADS, DH)
    )

    grad_all = lax.all_gather(d_att_b, "seq", axis=0, tiled=True)
    d_raw_b = score_grads(raw_scores, mask, d_att_b, value_all, divisor)
    d_query = jnp.einsum("hrc,chd->rhd", d_raw_b, key_all, preferred_element_type=jnp.float32)
    key_mask = visible(all_pos, all_seg, positions, segment, target)
    key_scores, key_attn_b = weights_of(query_all, key_b, key_mask, divisor)
    key_raw_b = score_grads(key_scores, key_mask, grad_all, value_b, divisor)
    d_key = jnp.einsum("hrc,rhd->chd", key_raw_b, query_all, preferred_element_type=jnp.float32)
    d_value = jnp.einsum("hrc,rhd->chd", key_attn_b, grad_all, preferred_element_type=jnp.float32)
    d_hidden = jnp.concatenate(
        [
            d_gate,
            d_value.reshape(rows, width),
            d_query.reshape(rows, width),
            d_key.reshape(rows, width),
        ],
        axis=1,
    )
    d_pre_b = (d_hidden * silu_slope(pre_act)).astype(jnp.bfloat16)
    in_part = jnp.dot(normed_b.T, d_pre_b, preferred_element_type=jnp.float32)
    d_normed = jnp.dot(d_pre_b, w_in.T, preferred_element_type=jnp.float32)
    d_x = (d_total + norm_back(d_normed, normed, inverse)).astype(jnp.bfloat16)
    partial_sums = (
        lax.psum_scatter(in_part, "seq", scatter_dimension=0, tiled=True),
        lax.psum_scatter(out_part, "seq", scatter_dimension=0, tiled=True),
        lax.psum_scatter(score_part, "seq", scatter_dimension=0, tiled=True),
    )
    d_w_in, d_w_out, d_w_score = (
        lax.psum_scatter(partial_sums[0], "dp", scatter_dimension=1, tiled=True),
        lax.psum_scatter(partial_sums[1], "dp", scatter_dimension=1, tiled=True),
        lax.psum_scatter(partial_sums[2], "dp", scatter_dimension=1, tiled=True),
    )
    d_head = lax.psum(head_part, ("dp", "seq"))
    return (d_x[None], d_w_in, d_w_out, d_w_score, d_head)


def solution(mesh):
    placed = (
        P("dp", "seq", None),
        P("dp", None),
        P("dp", None),
        P(),
        P(),
        P(),
        P(),
        P("dp", "seq", None),
        P("dp", "seq"),
    )
    return jax.shard_map(
        on_device,
        mesh=mesh,
        in_specs=placed,
        out_specs=(P("dp", "seq", None), P("seq", "dp"), P("seq", "dp"), P("seq", "dp"), P()),
        check_vma=False,
    )
```

```python
import functools

import jax
import jax.numpy as jnp
from jax import lax
from jax.experimental import pallas as pl
from jax.experimental.pallas import tpu as pltpu
from jax.sharding import PartitionSpec as P

HEADS = 4
DH = 128


NORM_EPS = 1e-05


def exchange_kernel(plan, *refs):
    count = len(plan)
    sources, targets = refs[:count], refs[count : 2 * count]
    send_sems, recv_sems, own_sems = refs[2 * count :]
    axes = sorted({axis for kind, axis in plan})
    barrier = pltpu.get_barrier_semaphore()
    for axis in axes:
        size, me = lax.axis_size(axis), lax.axis_index(axis)
        for step in range(1, size):
            pl.semaphore_signal(
                barrier,
                inc=1,
                device_id={axis: lax.rem(me + step, size)},
                device_id_type=pl.DeviceIdType.MESH,
            )
    pl.semaphore_wait(barrier, sum(lax.axis_size(axis) - 1 for axis in axes))

    def remote(source, target, number, slot, axis, peer):
        return pltpu.make_async_remote_copy(
            src_ref=source,
            dst_ref=target,
            send_sem=send_sems.at[number, slot],
            recv_sem=recv_sems.at[number, slot],
            device_id={axis: peer},
            device_id_type=pl.DeviceIdType.MESH,
        )

    sent, own, relays, landing = [], [], [], []
    for number, (kind, axis) in enumerate(plan):
        source, target = sources[number], targets[number]
        size, me = lax.axis_size(axis), lax.axis_index(axis)
        mine = source if kind == "gather" else source.at[me]
        own.append(pltpu.make_async_copy(mine, target.at[me], own_sems.at[number]))
        own[-1].start()
        if kind == "gather":
            sibling = me + 1 - 2 * lax.rem(me, 2)
            for step in range(1, size // 2):
                copy = remote(
                    source, target.at[me], number, step, axis, lax.rem(me + 2 * step, size)
                )
                copy.start()
                sent.append(copy)
                relays.append((number, axis, step, lax.rem(me + size - 2 * step, size), sibling))
            copy = remote(source, target.at[me], number, 0, axis, sibling)
            copy.start()
            sent.append(copy)
            landing.append(remote(source, target.at[sibling], number, 0, axis, sibling))
            for step in range(1, size // 2):
                origin = lax.rem(sibling + size - 2 * step, size)
                landing.append(
                    remote(source, target.at[origin], number, size // 2 + step, axis, sibling)
                )
        else:
            for step in range(1, size):
                peer = lax.rem(me + step, size)
                copy = remote(source.at[peer], target.at[me], number, step, axis, peer)
                copy.start()
                sent.append(copy)
                origin = lax.rem(me + size - step, size)
                landing.append(
                    remote(source.at[origin], target.at[origin], number, step, axis, origin)
                )
    for number, axis, step, origin, sibling in relays:
        size = lax.axis_size(axis)
        block = targets[number].at[origin]
        remote(sources[number], block, number, step, axis, origin).wait_recv()
        copy = remote(block, block, number, size // 2 + step, axis, sibling)
        copy.start()
        sent.append(copy)
    for copy in landing:
        copy.wait_recv()
    for copy in sent:
        copy.wait_send()
    for copy in own:
        copy.wait()


def exchange(identity, *items):
    plan = tuple((kind, axis) for kind, axis, array in items)
    arrays = [array for kind, axis, array in items]
    shapes = [
        jax.ShapeDtypeStruct(
            ((lax.axis_size(axis),) + array.shape) if kind == "gather" else array.shape,
            array.dtype,
        )
        for kind, axis, array in items
    ]
    slots = max(lax.axis_size(axis) for kind, axis in plan)
    return pl.pallas_call(
        functools.partial(exchange_kernel, plan),
        out_shape=shapes,
        in_specs=[pl.BlockSpec(memory_space=pl.ANY)] * len(arrays),
        out_specs=[pl.BlockSpec(memory_space=pl.ANY)] * len(arrays),
        scratch_shapes=[
            pltpu.SemaphoreType.DMA((len(arrays), slots)),
            pltpu.SemaphoreType.DMA((len(arrays), slots)),
            pltpu.SemaphoreType.DMA((len(arrays),)),
        ],
        compiler_params=pltpu.CompilerParams(collective_id=identity, has_side_effects=True),
    )(*arrays)


def blocks(array, count):
    rows, columns = array.shape
    return array.reshape(rows, count, columns // count).transpose(1, 0, 2)


def merged(array):
    return array.reshape(array.shape[0] * array.shape[1], array.shape[2])


def group_sum(array):
    return jnp.sum(array.astype(jnp.float32), axis=0)


def silu_slope(value):
    sigma = jax.nn.sigmoid(value)
    return sigma * (1.0 + value * (1.0 - sigma))


def norm_rows(value):
    centre = value - jnp.mean(value, axis=-1, keepdims=True)
    inverse = lax.rsqrt(jnp.mean(centre * centre, axis=-1, keepdims=True) + NORM_EPS)
    return (centre * inverse, inverse)


def norm_back(grad, normed, inverse):
    return inverse * (
        grad
        - jnp.mean(grad, axis=-1, keepdims=True)
        - normed * jnp.mean(grad * normed, axis=-1, keepdims=True)
    )


def row_marks(positions, lengths, targets):
    ends = jnp.cumsum(lengths)
    starts = ends - lengths
    counts = jnp.minimum(targets, lengths - 1)
    inside = (positions[:, None] >= starts[None, :]) & (positions[:, None] < ends[None, :])
    segment = jnp.sum((positions[:, None] >= ends[None, :]).astype(jnp.int32), axis=1)
    first_target = jnp.sum(jnp.where(inside, (ends - counts)[None, :], 0), axis=1)
    return (segment, positions >= first_target)


def visible(query_pos, query_seg, key_pos, key_seg, key_tgt):
    same_hist = query_seg[:, None] == key_seg[None, :]
    causal = key_pos[None, :] <= query_pos[:, None]
    open_key = jnp.logical_not(key_tgt)[None, :] | (key_pos[None, :] == query_pos[:, None])
    return (same_hist & causal & open_key)[None, :, :]


def weights_of(query_b, key_b, mask, divisor):
    raw_scores = jnp.einsum(
        "rhd,chd->hrc", query_b, key_b, preferred_element_type=jnp.float32
    ) * DH ** (-0.5)
    attn_b = jnp.where(mask, jax.nn.silu(raw_scores) / divisor, 0.0).astype(jnp.bfloat16)
    return (raw_scores, attn_b)


def score_grads(raw_scores, mask, grad_b, value_b, divisor):
    grad_attn = jnp.einsum("rhd,chd->hrc", grad_b, value_b, preferred_element_type=jnp.float32)
    factor = jnp.where(mask, silu_slope(raw_scores) * DH ** (-0.5) / divisor, 0.0)
    return (grad_attn * factor).astype(jnp.bfloat16)


def on_device(x_rows, lengths, targets, w_in, w_out, w_score, head_score, grad_out, grad_score):
    rows = x_rows.shape[1]
    seq_count = lax.axis_size("seq")
    total = rows * seq_count
    width = w_out.shape[0]
    divisor = float(total // 2)
    hist_len = lengths[0]
    hist_tgt = targets[0]
    own_start = lax.axis_index("seq") * rows
    positions = own_start + jnp.arange(rows, dtype=jnp.int32)
    all_pos = jnp.arange(total, dtype=jnp.int32)
    segment, target = row_marks(positions, hist_len, hist_tgt)
    all_seg, all_tgt = row_marks(all_pos, hist_len, hist_tgt)
    x_float = x_rows[0].astype(jnp.float32)
    normed, inverse = norm_rows(x_float)
    normed_b = normed.astype(jnp.bfloat16)
    pre_act = jnp.dot(normed_b, w_in, preferred_element_type=jnp.float32)
    hidden_b = jax.nn.silu(pre_act).astype(jnp.bfloat16)
    gate_b = hidden_b[:, 0:width]
    value_b = hidden_b[:, width : 2 * width].reshape(rows, HEADS, DH)
    query_b = hidden_b[:, 2 * width : 3 * width].reshape(rows, HEADS, DH)
    key_b = hidden_b[:, 3 * width : 4 * width].reshape(rows, HEADS, DH)
    moved, normed_cols = exchange(
        1,
        ("gather", "seq", hidden_b[:, width:]),
        ("swap", "seq", blocks(normed_b, seq_count)),
    )
    moved = merged(moved)
    value_all, query_all, key_all = (
        moved[:, at * width : (at + 1) * width].reshape(total, HEADS, DH) for at in range(3)
    )
    mask = visible(positions, segment, all_pos, all_seg, all_tgt)
    raw_scores, attn_b = weights_of(query_b, key_all, mask, divisor)
    attended = jnp.einsum("hrc,chd->rhd", attn_b, value_all, preferred_element_type=jnp.float32)
    attended = attended.reshape(rows, width)
    onorm, att_inverse = norm_rows(attended)
    gate_f = gate_b.astype(jnp.float32)
    gated_b = (onorm * gate_f).astype(jnp.bfloat16)
    output = x_float + jnp.dot(gated_b, w_out, preferred_element_type=jnp.float32)
    out_b = output.astype(jnp.bfloat16)
    mid_act = jnp.dot(out_b, w_score, preferred_element_type=jnp.float32)
    weight_c = grad_score[0] * target.astype(jnp.float32)
    head_part = jnp.sum(weight_c[:, None] * jax.nn.silu(mid_act), axis=0)
    d_mid_b = (weight_c[:, None] * head_score[None, :] * silu_slope(mid_act)).astype(jnp.bfloat16)
    d_total = grad_out[0].astype(jnp.float32) + jnp.dot(
        d_mid_b, w_score.T, preferred_element_type=jnp.float32
    )
    d_total_b = d_total.astype(jnp.bfloat16)
    d_gated = jnp.dot(d_total_b, w_out.T, preferred_element_type=jnp.float32)
    d_gate = d_gated * onorm
    d_att_b = (
        norm_back(d_gated * gate_f, onorm, att_inverse)
        .astype(jnp.bfloat16)
        .reshape(rows, HEADS, DH)
    )

    grad_all, total_all, mid_all, head_all, gated_cols, out_cols = exchange(
        2,
        ("gather", "seq", d_att_b.reshape(rows, width)),
        ("gather", "seq", d_total_b),
        ("gather", "seq", d_mid_b),
        ("gather", "seq", jnp.broadcast_to(head_part, (8, head_part.shape[0]))),
        ("swap", "seq", blocks(gated_b, seq_count)),
        ("swap", "seq", blocks(out_b, seq_count)),
    )
    grad_all = grad_all.reshape(total, HEADS, DH)
    out_part = jnp.dot(
        merged(gated_cols).T, merged(total_all), preferred_element_type=jnp.float32
    )
    score_part = jnp.dot(merged(out_cols).T, merged(mid_all), preferred_element_type=jnp.float32)
    head_group = jnp.sum(head_all, axis=0)
    d_raw_b = score_grads(raw_scores, mask, d_att_b, value_all, divisor)
    d_query = jnp.einsum("hrc,chd->rhd", d_raw_b, key_all, preferred_element_type=jnp.float32)
    key_mask = visible(all_pos, all_seg, positions, segment, target)
    key_scores, key_attn_b = weights_of(query_all, key_b, key_mask, divisor)
    key_raw_b = score_grads(key_scores, key_mask, grad_all, value_b, divisor)
    d_key = jnp.einsum("hrc,rhd->chd", key_raw_b, query_all, preferred_element_type=jnp.float32)
    d_value = jnp.einsum("hrc,rhd->chd", key_attn_b, grad_all, preferred_element_type=jnp.float32)
    d_hidden = jnp.concatenate(
        [
            d_gate,
            d_value.reshape(rows, width),
            d_query.reshape(rows, width),
            d_key.reshape(rows, width),
        ],
        axis=1,
    )
    d_pre_b = (d_hidden * silu_slope(pre_act)).astype(jnp.bfloat16)
    group_count = lax.axis_size("dp")
    pre_all, out_parts, score_parts, head_parts = exchange(
        3,
        ("gather", "seq", d_pre_b),
        ("swap", "dp", blocks(out_part.astype(jnp.bfloat16), group_count)),
        ("swap", "dp", blocks(score_part.astype(jnp.bfloat16), group_count)),
        ("swap", "dp", jnp.broadcast_to(head_group, (group_count,) + head_group.shape)),
    )
    in_part = jnp.dot(merged(normed_cols).T, merged(pre_all), preferred_element_type=jnp.float32)
    (in_parts,) = exchange(4, ("swap", "dp", blocks(in_part.astype(jnp.bfloat16), group_count)))
    d_normed = jnp.dot(d_pre_b, w_in.T, preferred_element_type=jnp.float32)
    d_x = (d_total + norm_back(d_normed, normed, inverse)).astype(jnp.bfloat16)
    return (
        d_x[None],
        group_sum(in_parts),
        group_sum(out_parts),
        group_sum(score_parts),
        group_sum(head_parts)[0],
    )


def solution(mesh):
    placed = (
        P("dp", "seq", None),
        P("dp", None),
        P("dp", None),
        P(),
        P(),
        P(),
        P(),
        P("dp", "seq", None),
        P("dp", "seq"),
    )
    return jax.shard_map(
        on_device,
        mesh=mesh,
        in_specs=placed,
        out_specs=(P("dp", "seq", None), P("seq", "dp"), P("seq", "dp"), P("seq", "dp"), P()),
        check_vma=False,
    )
```

```python
import functools

import jax
import jax.numpy as jnp
from jax import lax
from jax.experimental import pallas as pl
from jax.experimental.pallas import tpu as pltpu
from jax.sharding import PartitionSpec as P

HEADS = 4
DH = 128


NORM_EPS = 1e-05


def exchange_kernel(plan, *refs):
    count = len(plan)
    sources, targets = refs[:count], refs[count : 2 * count]
    send_sems, recv_sems, own_sems = refs[2 * count :]
    axes = sorted({axis for kind, axis in plan})
    barrier = pltpu.get_barrier_semaphore()
    for axis in axes:
        size, me = lax.axis_size(axis), lax.axis_index(axis)
        for step in range(1, size):
            pl.semaphore_signal(
                barrier,
                inc=1,
                device_id={axis: lax.rem(me + step, size)},
                device_id_type=pl.DeviceIdType.MESH,
            )
    pl.semaphore_wait(barrier, sum(lax.axis_size(axis) - 1 for axis in axes))

    def remote(source, target, number, slot, axis, peer):
        return pltpu.make_async_remote_copy(
            src_ref=source,
            dst_ref=target,
            send_sem=send_sems.at[number, slot],
            recv_sem=recv_sems.at[number, slot],
            device_id={axis: peer},
            device_id_type=pl.DeviceIdType.MESH,
        )

    sent, own, relays, landing = [], [], [], []
    for number, (kind, axis) in enumerate(plan):
        source, target = sources[number], targets[number]
        size, me = lax.axis_size(axis), lax.axis_index(axis)
        mine = source if kind == "gather" else source.at[me]
        own.append(pltpu.make_async_copy(mine, target.at[me], own_sems.at[number]))
        own[-1].start()
        if kind == "gather":
            sibling = me + 1 - 2 * lax.rem(me, 2)
            for step in range(1, size // 2):
                copy = remote(
                    source, target.at[me], number, step, axis, lax.rem(me + 2 * step, size)
                )
                copy.start()
                sent.append(copy)
                relays.append((number, axis, step, lax.rem(me + size - 2 * step, size), sibling))
            copy = remote(source, target.at[me], number, 0, axis, sibling)
            copy.start()
            sent.append(copy)
            landing.append(remote(source, target.at[sibling], number, 0, axis, sibling))
            for step in range(1, size // 2):
                origin = lax.rem(sibling + size - 2 * step, size)
                landing.append(
                    remote(source, target.at[origin], number, size // 2 + step, axis, sibling)
                )
        else:
            for step in range(1, size):
                peer = lax.rem(me + step, size)
                copy = remote(source.at[peer], target.at[me], number, step, axis, peer)
                copy.start()
                sent.append(copy)
                origin = lax.rem(me + size - step, size)
                landing.append(
                    remote(source.at[origin], target.at[origin], number, step, axis, origin)
                )
    for number, axis, step, origin, sibling in relays:
        size = lax.axis_size(axis)
        block = targets[number].at[origin]
        remote(sources[number], block, number, step, axis, origin).wait_recv()
        copy = remote(block, block, number, size // 2 + step, axis, sibling)
        copy.start()
        sent.append(copy)
    for copy in landing:
        copy.wait_recv()
    for copy in sent:
        copy.wait_send()
    for copy in own:
        copy.wait()


def exchange(identity, *items):
    plan = tuple((kind, axis) for kind, axis, array in items)
    arrays = [array for kind, axis, array in items]
    shapes = [
        jax.ShapeDtypeStruct(
            ((lax.axis_size(axis),) + array.shape) if kind == "gather" else array.shape,
            array.dtype,
        )
        for kind, axis, array in items
    ]
    slots = max(lax.axis_size(axis) for kind, axis in plan)
    return pl.pallas_call(
        functools.partial(exchange_kernel, plan),
        out_shape=shapes,
        in_specs=[pl.BlockSpec(memory_space=pl.ANY)] * len(arrays),
        out_specs=[pl.BlockSpec(memory_space=pl.ANY)] * len(arrays),
        scratch_shapes=[
            pltpu.SemaphoreType.DMA((len(arrays), slots)),
            pltpu.SemaphoreType.DMA((len(arrays), slots)),
            pltpu.SemaphoreType.DMA((len(arrays),)),
        ],
        compiler_params=pltpu.CompilerParams(collective_id=identity, has_side_effects=True),
    )(*arrays)


def blocks(array, count):
    rows, columns = array.shape
    return array.reshape(rows, count, columns // count).transpose(1, 0, 2)


def merged(array):
    return array.reshape(array.shape[0] * array.shape[1], array.shape[2])


def group_sum(array):
    return jnp.sum(array.astype(jnp.float32), axis=0)


def silu_slope(value):
    sigma = jax.nn.sigmoid(value)
    return sigma * (1.0 + value * (1.0 - sigma))


def norm_rows(value):
    centre = value - jnp.mean(value, axis=-1, keepdims=True)
    inverse = lax.rsqrt(jnp.mean(centre * centre, axis=-1, keepdims=True) + NORM_EPS)
    return (centre * inverse, inverse)


def norm_back(grad, normed, inverse):
    return inverse * (
        grad
        - jnp.mean(grad, axis=-1, keepdims=True)
        - normed * jnp.mean(grad * normed, axis=-1, keepdims=True)
    )


def marks(positions, lengths, targets):
    start = jnp.zeros_like(positions)
    first = jnp.zeros_like(positions)
    end = 0
    for number in range(lengths.shape[1]):
        length = lengths[0, number]
        begin, end = end, end + length
        inside = (positions >= begin) & (positions < end)
        start = jnp.where(inside, begin, start)
        first = jnp.where(inside, end - jnp.minimum(targets[0, number], length - 1), first)
    return start, positions >= first


def seen(query_pos, query_start, key_pos, key_tgt):
    same = (key_pos <= query_pos) & (key_pos >= query_start)
    return same & (jnp.logical_not(key_tgt) | (key_pos == query_pos))


def nt_dot(left, right):
    return lax.dot_general(
        left, right, (((1,), (1,)), ((), ())), preferred_element_type=jnp.float32
    )


def nn_dot(left, right):
    return jnp.dot(left, right, preferred_element_type=jnp.float32)


def store_blocks(target, value):
    width = target.shape[2]
    for number in range(target.shape[0]):
        target[number] = value[:, number * width : (number + 1) * width]


def head_cols(ref, column):
    part = ref[:, :, column : column + DH]
    return part.reshape(part.shape[0] * part.shape[1], DH)


def opening_kernel(x_ref, w_in_ref, normed_ref, pre_ref, gate_ref, rest_ref):
    normed, inverse = norm_rows(x_ref[...].astype(jnp.float32))
    normed_b = normed.astype(jnp.bfloat16)
    store_blocks(normed_ref, normed_b)
    width = gate_ref.shape[1]
    for number in range(4):
        columns = slice(number * width, (number + 1) * width)
        pre = nn_dot(normed_b, w_in_ref[:, columns])
        pre_ref[:, columns] = pre
        hidden_b = jax.nn.silu(pre).astype(jnp.bfloat16)
        if number == 0:
            gate_ref[...] = hidden_b
        else:
            rest_ref[:, (number - 1) * width : number * width] = hidden_b


def middle_kernel(
    divisor,
    lengths,
    targets,
    own_start,
    moved_ref,
    own_ref,
    gate_ref,
    pre_ref,
    x_ref,
    grad_ref,
    score_ref,
    head_score_ref,
    w_out_ref,
    w_score_ref,
    d_att_ref,
    d_total_ref,
    d_total_b_ref,
    d_mid_ref,
    head_ref,
    gated_ref,
    out_ref,
    d_pre_ref,
    attended_ref,
):
    rows, width = gate_ref.shape
    total = moved_ref.shape[0] * rows
    query_pos = own_start[0] + lax.broadcasted_iota(jnp.int32, (rows, 1), 0)
    key_pos = lax.broadcasted_iota(jnp.int32, (1, total), 1)
    query_start, query_tgt = marks(query_pos, lengths, targets)
    unused, key_tgt = marks(key_pos, lengths, targets)
    mask = seen(query_pos, query_start, key_pos, key_tgt)
    for head in range(HEADS):
        column = head * DH
        query = own_ref[:, width + column : width + column + DH]
        raw = nt_dot(query, head_cols(moved_ref, 2 * width + column)) * DH ** (-0.5)
        attn_b = jnp.where(mask, jax.nn.silu(raw) / divisor, 0.0).astype(jnp.bfloat16)
        attended_ref[:, column : column + DH] = nn_dot(attn_b, head_cols(moved_ref, column))
    onorm, att_inverse = norm_rows(attended_ref[...])
    gate_f = gate_ref[...].astype(jnp.float32)
    gated_b = (onorm * gate_f).astype(jnp.bfloat16)
    store_blocks(gated_ref, gated_b)
    output = x_ref[...].astype(jnp.float32) + nn_dot(gated_b, w_out_ref[...])
    out_b = output.astype(jnp.bfloat16)
    store_blocks(out_ref, out_b)
    mid_act = nn_dot(out_b, w_score_ref[...])
    weight_c = score_ref[...] * query_tgt.astype(jnp.float32)
    head_part = jnp.sum(weight_c * jax.nn.silu(mid_act), axis=0, keepdims=True)
    head_ref[...] = jnp.broadcast_to(head_part, head_ref.shape)
    d_mid_b = (weight_c * head_score_ref[...] * silu_slope(mid_act)).astype(jnp.bfloat16)
    d_mid_ref[...] = d_mid_b
    d_total = grad_ref[...].astype(jnp.float32) + nt_dot(d_mid_b, w_score_ref[...])
    d_total_ref[...] = d_total
    d_total_b = d_total.astype(jnp.bfloat16)
    d_total_b_ref[...] = d_total_b
    d_gated = nt_dot(d_total_b, w_out_ref[...])
    d_pre_ref[...] = (d_gated * onorm * silu_slope(pre_ref[:, 0:width])).astype(jnp.bfloat16)
    d_att_ref[...] = norm_back(d_gated * gate_f, onorm, att_inverse).astype(jnp.bfloat16)


def closing_kernel(
    divisor,
    lengths,
    targets,
    own_start,
    moved_ref,
    grad_all_ref,
    own_ref,
    own_grad_ref,
    pre_ref,
    d_pre_gate_ref,
    x_ref,
    d_total_ref,
    w_in_ref,
    d_pre_ref,
    d_x_ref,
):
    rows, width = own_grad_ref.shape
    total = moved_ref.shape[0] * rows
    own_col = own_start[0] + lax.broadcasted_iota(jnp.int32, (rows, 1), 0)
    all_row = lax.broadcasted_iota(jnp.int32, (1, total), 1)
    own_first, own_tgt = marks(own_col, lengths, targets)
    all_first, all_tgt = marks(all_row, lengths, targets)
    mask = seen(own_col, own_first, all_row, all_tgt)
    key_mask = seen(all_row, all_first, own_col, own_tgt)
    scale = DH ** (-0.5)

    def store(kind, column, value):
        columns = slice(kind * width + column, kind * width + column + DH)
        slope = silu_slope(pre_ref[:, columns])
        d_pre_ref[:, columns] = (value * slope).astype(jnp.bfloat16)

    d_pre_ref[:, 0:width] = d_pre_gate_ref[...]
    for head in range(HEADS):
        column = head * DH
        value_own = own_ref[:, column : column + DH]
        query_own = own_ref[:, width + column : width + column + DH]
        key_own = own_ref[:, 2 * width + column : 2 * width + column + DH]
        grad_own = own_grad_ref[:, column : column + DH]
        value_all = head_cols(moved_ref, column)
        query_all = head_cols(moved_ref, width + column)
        key_all = head_cols(moved_ref, 2 * width + column)
        grad_all = head_cols(grad_all_ref, column)
        raw = nt_dot(query_own, key_all) * scale
        factor = jnp.where(mask, silu_slope(raw) * scale / divisor, 0.0)
        d_raw_b = (nt_dot(grad_own, value_all) * factor).astype(jnp.bfloat16)
        store(2, column, nn_dot(d_raw_b, key_all))
        raw = nt_dot(key_own, query_all) * scale
        sigma = jax.nn.sigmoid(raw)
        attn_b = jnp.where(key_mask, raw * sigma / divisor, 0.0).astype(jnp.bfloat16)
        slope = sigma * (1.0 + raw * (1.0 - sigma))
        factor = jnp.where(key_mask, slope * scale / divisor, 0.0)
        d_raw_b = (nt_dot(value_own, grad_all) * factor).astype(jnp.bfloat16)
        store(3, column, nn_dot(d_raw_b, query_all))
        store(1, column, nn_dot(attn_b, grad_all))
    normed, inverse = norm_rows(x_ref[...].astype(jnp.float32))
    d_normed = nt_dot(d_pre_ref[...], w_in_ref[...])
    d_x = d_total_ref[...] + norm_back(d_normed, normed, inverse)
    d_x_ref[...] = d_x.astype(jnp.bfloat16)


def local_call(kernel, scalars, arrays, outs, scratch=()):
    return pl.pallas_call(
        kernel,
        out_shape=[jax.ShapeDtypeStruct(shape, kind) for shape, kind in outs],
        in_specs=[pl.BlockSpec(memory_space=pltpu.SMEM)] * len(scalars)
        + [pl.BlockSpec(memory_space=pltpu.VMEM)] * len(arrays),
        out_specs=[pl.BlockSpec(memory_space=pltpu.VMEM)] * len(outs),
        scratch_shapes=list(scratch),
        compiler_params=pltpu.CompilerParams(vmem_limit_bytes=56 * 1024 * 1024),
    )(*scalars, *arrays)


def on_device(x_rows, lengths, targets, w_in, w_out, w_score, head_score, grad_out, grad_score):
    rows, features = x_rows.shape[1:]
    seq_count = lax.axis_size("seq")
    group_count = lax.axis_size("dp")
    total = rows * seq_count
    width = w_out.shape[0]
    middle = head_score.shape[0]
    divisor = float(total // 2)
    half, full = jnp.bfloat16, jnp.float32
    own_start = (lax.axis_index("seq") * rows).astype(jnp.int32)[None]
    scalars = (lengths, targets, own_start)
    normed_blocks, pre_act, gate_b, own_b = local_call(
        opening_kernel,
        (),
        (x_rows[0], w_in),
        (
            ((seq_count, rows, features // seq_count), half),
            ((rows, 4 * width), full),
            ((rows, width), half),
            ((rows, 3 * width), half),
        ),
    )
    moved, normed_cols = exchange(
        1, ("gather", "seq", own_b), ("swap", "seq", normed_blocks)
    )
    d_att_b, d_total, d_total_b, d_mid_b, head_part, gated_blocks, out_blocks, d_pre_gate = (
        local_call(
            functools.partial(middle_kernel, divisor),
            scalars,
            (
                moved,
                own_b,
                gate_b,
                pre_act,
                x_rows[0],
                grad_out[0],
                grad_score[0][:, None],
                head_score[None, :],
                w_out,
                w_score,
            ),
            (
                ((rows, width), half),
                ((rows, features), full),
                ((rows, features), half),
                ((rows, middle), half),
                ((8, middle), full),
                ((seq_count, rows, width // seq_count), half),
                ((seq_count, rows, features // seq_count), half),
                ((rows, width), half),
            ),
            (pltpu.VMEM((rows, width), full),),
        )
    )
    grad_all, total_all, mid_all, head_all, gated_cols, out_cols = exchange(
        2,
        ("gather", "seq", d_att_b),
        ("gather", "seq", d_total_b),
        ("gather", "seq", d_mid_b),
        ("gather", "seq", head_part),
        ("swap", "seq", gated_blocks),
        ("swap", "seq", out_blocks),
    )
    out_part = nn_dot(merged(gated_cols).T, merged(total_all))
    score_part = nn_dot(merged(out_cols).T, merged(mid_all))
    head_group = jnp.sum(head_all, axis=0)
    d_pre_b, d_x = local_call(
        functools.partial(closing_kernel, divisor),
        scalars,
        (moved, grad_all, own_b, d_att_b, pre_act, d_pre_gate, x_rows[0], d_total, w_in),
        (((rows, 4 * width), half), ((rows, features), half)),
    )
    pre_all, out_parts, score_parts, head_parts = exchange(
        3,
        ("gather", "seq", d_pre_b),
        ("swap", "dp", blocks(out_part.astype(half), group_count)),
        ("swap", "dp", blocks(score_part.astype(half), group_count)),
        ("swap", "dp", jnp.broadcast_to(head_group, (group_count,) + head_group.shape)),
    )
    in_part = nn_dot(merged(normed_cols).T, merged(pre_all))
    (in_parts,) = exchange(4, ("swap", "dp", blocks(in_part.astype(half), group_count)))
    return (
        d_x[None],
        group_sum(in_parts),
        group_sum(out_parts),
        group_sum(score_parts),
        group_sum(head_parts)[0],
    )


def solution(mesh):
    placed = (
        P("dp", "seq", None),
        P("dp", None),
        P("dp", None),
        P(),
        P(),
        P(),
        P(),
        P("dp", "seq", None),
        P("dp", "seq"),
    )
    return jax.shard_map(
        on_device,
        mesh=mesh,
        in_specs=placed,
        out_specs=(P("dp", "seq", None), P("seq", "dp"), P("seq", "dp"), P("seq", "dp"), P()),
        check_vma=False,
    )
```

```python
import functools

import jax
import jax.numpy as jnp
from jax import lax
from jax.experimental import pallas as pl
from jax.experimental.pallas import tpu as pltpu
from jax.sharding import PartitionSpec as P

HEADS = 4
DH = 128


NORM_EPS = 1e-05


def exchange_kernel(plan, *refs):
    count = len(plan)
    sources, targets = refs[:count], refs[count : 2 * count]
    send_sems, recv_sems, own_sems = refs[2 * count :]
    axes = sorted({axis for kind, axis in plan})
    barrier = pltpu.get_barrier_semaphore()
    for axis in axes:
        size, me = lax.axis_size(axis), lax.axis_index(axis)
        for step in range(1, size):
            pl.semaphore_signal(
                barrier,
                inc=1,
                device_id={axis: lax.rem(me + step, size)},
                device_id_type=pl.DeviceIdType.MESH,
            )
    pl.semaphore_wait(barrier, sum(lax.axis_size(axis) - 1 for axis in axes))

    def remote(source, target, number, slot, axis, peer):
        return pltpu.make_async_remote_copy(
            src_ref=source,
            dst_ref=target,
            send_sem=send_sems.at[number, slot],
            recv_sem=recv_sems.at[number, slot],
            device_id={axis: peer},
            device_id_type=pl.DeviceIdType.MESH,
        )

    sent, own, relays, landing = [], [], [], []
    for number, (kind, axis) in enumerate(plan):
        source, target = sources[number], targets[number]
        size, me = lax.axis_size(axis), lax.axis_index(axis)
        mine = source if kind == "gather" else source.at[me]
        own.append(pltpu.make_async_copy(mine, target.at[me], own_sems.at[number]))
        own[-1].start()
        if kind == "gather":
            sibling = me + 1 - 2 * lax.rem(me, 2)
            for step in range(1, size // 2):
                copy = remote(
                    source, target.at[me], number, step, axis, lax.rem(me + 2 * step, size)
                )
                copy.start()
                sent.append(copy)
                relays.append((number, axis, step, lax.rem(me + size - 2 * step, size), sibling))
            copy = remote(source, target.at[me], number, 0, axis, sibling)
            copy.start()
            sent.append(copy)
            landing.append(remote(source, target.at[sibling], number, 0, axis, sibling))
            for step in range(1, size // 2):
                origin = lax.rem(sibling + size - 2 * step, size)
                landing.append(
                    remote(source, target.at[origin], number, size // 2 + step, axis, sibling)
                )
        else:
            for step in range(1, size):
                peer = lax.rem(me + step, size)
                copy = remote(source.at[peer], target.at[me], number, step, axis, peer)
                copy.start()
                sent.append(copy)
                origin = lax.rem(me + size - step, size)
                landing.append(
                    remote(source.at[origin], target.at[origin], number, step, axis, origin)
                )
    for number, axis, step, origin, sibling in relays:
        size = lax.axis_size(axis)
        block = targets[number].at[origin]
        remote(sources[number], block, number, step, axis, origin).wait_recv()
        copy = remote(block, block, number, size // 2 + step, axis, sibling)
        copy.start()
        sent.append(copy)
    for copy in landing:
        copy.wait_recv()
    for copy in sent:
        copy.wait_send()
    for copy in own:
        copy.wait()


def exchange(identity, *items):
    plan = tuple((kind, axis) for kind, axis, array in items)
    arrays = [array for kind, axis, array in items]
    shapes = [
        jax.ShapeDtypeStruct(
            ((lax.axis_size(axis),) + array.shape) if kind == "gather" else array.shape,
            array.dtype,
        )
        for kind, axis, array in items
    ]
    slots = max(lax.axis_size(axis) for kind, axis in plan)
    return pl.pallas_call(
        functools.partial(exchange_kernel, plan),
        out_shape=shapes,
        in_specs=[pl.BlockSpec(memory_space=pl.ANY)] * len(arrays),
        out_specs=[pl.BlockSpec(memory_space=pl.ANY)] * len(arrays),
        scratch_shapes=[
            pltpu.SemaphoreType.DMA((len(arrays), slots)),
            pltpu.SemaphoreType.DMA((len(arrays), slots)),
            pltpu.SemaphoreType.DMA((len(arrays),)),
        ],
        compiler_params=pltpu.CompilerParams(collective_id=identity, has_side_effects=True),
    )(*arrays)


def blocks(array, count):
    rows, columns = array.shape
    return array.reshape(rows, count, columns // count).transpose(1, 0, 2)


def merged(array):
    return array.reshape(array.shape[0] * array.shape[1], array.shape[2])


def group_sum(array):
    return jnp.sum(array.astype(jnp.float32), axis=0)


def silu_slope(value):
    sigma = jax.nn.sigmoid(value)
    return sigma * (1.0 + value * (1.0 - sigma))


def norm_rows(value):
    centre = value - jnp.mean(value, axis=-1, keepdims=True)
    inverse = lax.rsqrt(jnp.mean(centre * centre, axis=-1, keepdims=True) + NORM_EPS)
    return (centre * inverse, inverse)


def norm_back(grad, normed, inverse):
    return inverse * (
        grad
        - jnp.mean(grad, axis=-1, keepdims=True)
        - normed * jnp.mean(grad * normed, axis=-1, keepdims=True)
    )


def marks(positions, lengths, targets):
    start = jnp.zeros_like(positions)
    first = jnp.zeros_like(positions)
    end = 0
    for number in range(lengths.shape[1]):
        length = lengths[0, number]
        begin, end = end, end + length
        inside = (positions >= begin) & (positions < end)
        start = jnp.where(inside, begin, start)
        first = jnp.where(inside, end - jnp.minimum(targets[0, number], length - 1), first)
    return start, positions >= first


def seen(query_pos, query_start, key_pos, key_tgt):
    same = (key_pos <= query_pos) & (key_pos >= query_start)
    return same & (jnp.logical_not(key_tgt) | (key_pos == query_pos))


def nt_dot(left, right):
    return lax.dot_general(
        left, right, (((1,), (1,)), ((), ())), preferred_element_type=jnp.float32
    )


def nn_dot(left, right):
    return jnp.dot(left, right, preferred_element_type=jnp.float32)


def store_blocks(target, value):
    width = target.shape[2]
    for number in range(target.shape[0]):
        target[number] = value[:, number * width : (number + 1) * width]


def head_cols(ref, column):
    part = ref[:, :, column : column + DH]
    return part.reshape(part.shape[0] * part.shape[1], DH)


def opening_kernel(x_ref, w_in_ref, normed_ref, pre_ref, gate_ref, rest_ref):
    normed, inverse = norm_rows(x_ref[...].astype(jnp.float32))
    normed_b = normed.astype(jnp.bfloat16)
    store_blocks(normed_ref, normed_b)
    width = gate_ref.shape[1]
    for number in range(4):
        columns = slice(number * width, (number + 1) * width)
        pre = nn_dot(normed_b, w_in_ref[:, columns])
        pre_ref[:, columns] = pre
        hidden_b = jax.nn.silu(pre).astype(jnp.bfloat16)
        if number == 0:
            gate_ref[...] = hidden_b
        else:
            rest_ref[:, (number - 1) * width : number * width] = hidden_b


def middle_kernel(
    divisor,
    lengths,
    targets,
    own_start,
    moved_ref,
    own_ref,
    gate_ref,
    pre_ref,
    x_ref,
    grad_ref,
    score_ref,
    head_score_ref,
    w_out_ref,
    w_score_ref,
    d_att_ref,
    d_total_ref,
    early_ref,
    head_ref,
    gated_ref,
    out_ref,
    attended_ref,
):
    rows, width = gate_ref.shape
    total = moved_ref.shape[0] * rows
    query_pos = own_start[0] + lax.broadcasted_iota(jnp.int32, (rows, 1), 0)
    key_pos = lax.broadcasted_iota(jnp.int32, (1, total), 1)
    query_start, query_tgt = marks(query_pos, lengths, targets)
    unused, key_tgt = marks(key_pos, lengths, targets)
    mask = seen(query_pos, query_start, key_pos, key_tgt)
    for head in range(HEADS):
        column = head * DH
        query = own_ref[:, width + column : width + column + DH]
        raw = nt_dot(query, head_cols(moved_ref, 2 * width + column)) * DH ** (-0.5)
        attn_b = jnp.where(mask, jax.nn.silu(raw) / divisor, 0.0).astype(jnp.bfloat16)
        attended_ref[:, column : column + DH] = nn_dot(attn_b, head_cols(moved_ref, column))
    onorm, att_inverse = norm_rows(attended_ref[...])
    gate_f = gate_ref[...].astype(jnp.float32)
    gated_b = (onorm * gate_f).astype(jnp.bfloat16)
    store_blocks(gated_ref, gated_b)
    output = x_ref[...].astype(jnp.float32) + nn_dot(gated_b, w_out_ref[...])
    out_b = output.astype(jnp.bfloat16)
    store_blocks(out_ref, out_b)
    mid_act = nn_dot(out_b, w_score_ref[...])
    weight_c = score_ref[...] * query_tgt.astype(jnp.float32)
    head_part = jnp.sum(weight_c * jax.nn.silu(mid_act), axis=0, keepdims=True)
    head_ref[...] = jnp.broadcast_to(head_part, head_ref.shape)
    d_mid_b = (weight_c * head_score_ref[...] * silu_slope(mid_act)).astype(jnp.bfloat16)
    features, middle = x_ref.shape[1], d_mid_b.shape[1]
    early_ref[:, features : features + middle] = d_mid_b
    d_total = grad_ref[...].astype(jnp.float32) + nt_dot(d_mid_b, w_score_ref[...])
    d_total_ref[...] = d_total
    d_total_b = d_total.astype(jnp.bfloat16)
    early_ref[:, 0:features] = d_total_b
    d_gated = nt_dot(d_total_b, w_out_ref[...])
    d_pre_gate = d_gated * onorm * silu_slope(pre_ref[:, 0:width])
    early_ref[:, features + middle :] = d_pre_gate.astype(jnp.bfloat16)
    d_att_ref[...] = norm_back(d_gated * gate_f, onorm, att_inverse).astype(jnp.bfloat16)


def closing_kernel(
    divisor,
    lengths,
    targets,
    own_start,
    moved_ref,
    grad_all_ref,
    own_ref,
    own_grad_ref,
    pre_ref,
    early_ref,
    x_ref,
    d_total_ref,
    w_in_ref,
    d_pre_ref,
    d_x_ref,
):
    rows, width = own_grad_ref.shape
    total = moved_ref.shape[0] * rows
    own_col = own_start[0] + lax.broadcasted_iota(jnp.int32, (rows, 1), 0)
    all_row = lax.broadcasted_iota(jnp.int32, (1, total), 1)
    own_first, own_tgt = marks(own_col, lengths, targets)
    all_first, all_tgt = marks(all_row, lengths, targets)
    mask = seen(own_col, own_first, all_row, all_tgt)
    key_mask = seen(all_row, all_first, own_col, own_tgt)
    scale = DH ** (-0.5)

    def store(kind, column, value):
        first = kind * width + column
        slope = silu_slope(pre_ref[:, first : first + DH])
        d_pre_ref[:, first - width : first - width + DH] = (value * slope).astype(jnp.bfloat16)

    for head in range(HEADS):
        column = head * DH
        value_own = own_ref[:, column : column + DH]
        query_own = own_ref[:, width + column : width + column + DH]
        key_own = own_ref[:, 2 * width + column : 2 * width + column + DH]
        grad_own = own_grad_ref[:, column : column + DH]
        value_all = head_cols(moved_ref, column)
        query_all = head_cols(moved_ref, width + column)
        key_all = head_cols(moved_ref, 2 * width + column)
        grad_all = head_cols(grad_all_ref, column)
        raw = nt_dot(query_own, key_all) * scale
        factor = jnp.where(mask, silu_slope(raw) * scale / divisor, 0.0)
        d_raw_b = (nt_dot(grad_own, value_all) * factor).astype(jnp.bfloat16)
        store(2, column, nn_dot(d_raw_b, key_all))
        raw = nt_dot(key_own, query_all) * scale
        sigma = jax.nn.sigmoid(raw)
        attn_b = jnp.where(key_mask, raw * sigma / divisor, 0.0).astype(jnp.bfloat16)
        slope = sigma * (1.0 + raw * (1.0 - sigma))
        factor = jnp.where(key_mask, slope * scale / divisor, 0.0)
        d_raw_b = (nt_dot(value_own, grad_all) * factor).astype(jnp.bfloat16)
        store(3, column, nn_dot(d_raw_b, query_all))
        store(1, column, nn_dot(attn_b, grad_all))
    normed, inverse = norm_rows(x_ref[...].astype(jnp.float32))
    gate_at = early_ref.shape[1] - width
    d_normed = nt_dot(early_ref[:, gate_at:], w_in_ref[:, 0:width])
    d_normed = d_normed + nt_dot(d_pre_ref[...], w_in_ref[:, width:])
    d_x = d_total_ref[...] + norm_back(d_normed, normed, inverse)
    d_x_ref[...] = d_x.astype(jnp.bfloat16)


def local_call(kernel, scalars, arrays, outs, scratch=()):
    return pl.pallas_call(
        kernel,
        out_shape=[jax.ShapeDtypeStruct(shape, kind) for shape, kind in outs],
        in_specs=[pl.BlockSpec(memory_space=pltpu.SMEM)] * len(scalars)
        + [pl.BlockSpec(memory_space=pltpu.VMEM)] * len(arrays),
        out_specs=[pl.BlockSpec(memory_space=pltpu.VMEM)] * len(outs),
        scratch_shapes=list(scratch),
        compiler_params=pltpu.CompilerParams(vmem_limit_bytes=56 * 1024 * 1024),
    )(*scalars, *arrays)


def on_device(x_rows, lengths, targets, w_in, w_out, w_score, head_score, grad_out, grad_score):
    rows, features = x_rows.shape[1:]
    seq_count = lax.axis_size("seq")
    group_count = lax.axis_size("dp")
    total = rows * seq_count
    width = w_out.shape[0]
    middle = head_score.shape[0]
    divisor = float(total // 2)
    half, full = jnp.bfloat16, jnp.float32
    own_start = (lax.axis_index("seq") * rows).astype(jnp.int32)[None]
    scalars = (lengths, targets, own_start)
    normed_blocks, pre_act, gate_b, own_b = local_call(
        opening_kernel,
        (),
        (x_rows[0], w_in),
        (
            ((seq_count, rows, features // seq_count), half),
            ((rows, 4 * width), full),
            ((rows, width), half),
            ((rows, 3 * width), half),
        ),
    )
    moved, normed_cols = exchange(
        1, ("gather", "seq", own_b), ("swap", "seq", normed_blocks)
    )
    d_att_b, d_total, early_b, head_part, gated_blocks, out_blocks = (
        local_call(
            functools.partial(middle_kernel, divisor),
            scalars,
            (
                moved,
                own_b,
                gate_b,
                pre_act,
                x_rows[0],
                grad_out[0],
                grad_score[0][:, None],
                head_score[None, :],
                w_out,
                w_score,
            ),
            (
                ((rows, width), half),
                ((rows, features), full),
                ((rows, features + middle + width), half),
                ((8, middle), full),
                ((seq_count, rows, width // seq_count), half),
                ((seq_count, rows, features // seq_count), half),
            ),
            (pltpu.VMEM((rows, width), full),),
        )
    )
    early_all = lax.all_gather(early_b, "seq", axis=0, tiled=True)
    grad_all, head_all = exchange(
        2, ("gather", "seq", d_att_b), ("gather", "seq", head_part)
    )
    d_rest_b, d_x = local_call(
        functools.partial(closing_kernel, divisor),
        scalars,
        (moved, grad_all, own_b, d_att_b, pre_act, early_b, x_rows[0], d_total, w_in),
        (((rows, 3 * width), half), ((rows, features), half)),
    )
    rest_all, gated_cols, out_cols = exchange(
        3,
        ("gather", "seq", d_rest_b),
        ("swap", "seq", gated_blocks),
        ("swap", "seq", out_blocks),
    )
    out_part = nn_dot(merged(gated_cols).T, early_all[:, 0:features])
    score_part = nn_dot(merged(out_cols).T, early_all[:, features : features + middle])
    normed_t = merged(normed_cols).T
    in_part = jnp.concatenate(
        [nn_dot(normed_t, early_all[:, features + middle :]), nn_dot(normed_t, merged(rest_all))],
        axis=1,
    )
    head_group = jnp.sum(head_all, axis=0)
    in_parts, out_parts, score_parts, head_parts = exchange(
        4,
        ("swap", "dp", blocks(in_part.astype(half), group_count)),
        ("swap", "dp", blocks(out_part.astype(half), group_count)),
        ("swap", "dp", blocks(score_part.astype(half), group_count)),
        ("swap", "dp", jnp.broadcast_to(head_group, (group_count,) + head_group.shape)),
    )
    return (
        d_x[None],
        group_sum(in_parts),
        group_sum(out_parts),
        group_sum(score_parts),
        group_sum(head_parts)[0],
    )


def solution(mesh):
    placed = (
        P("dp", "seq", None),
        P("dp", None),
        P("dp", None),
        P(),
        P(),
        P(),
        P(),
        P("dp", "seq", None),
        P("dp", "seq"),
    )
    return jax.shard_map(
        on_device,
        mesh=mesh,
        in_specs=placed,
        out_specs=(P("dp", "seq", None), P("seq", "dp"), P("seq", "dp"), P("seq", "dp"), P()),
        check_vma=False,
    )
```

```python
import functools

import jax
import jax.numpy as jnp
from jax import lax
from jax.experimental import pallas as pl
from jax.experimental.pallas import tpu as pltpu
from jax.sharding import PartitionSpec as P

HEADS = 4
DH = 128


NORM_EPS = 1e-05


def flipped(index, bit):
    return index + bit - 2 * bit * lax.rem(index // bit, 2)


def exchange_kernel(plan, *refs):
    count = len(plan)
    sources, targets = refs[:count], refs[count : 2 * count]
    send_sems, recv_sems, own_sems = refs[2 * count :]
    axes = sorted({axis for kind, axis in plan})
    barrier = pltpu.get_barrier_semaphore()
    for axis in axes:
        size, me = lax.axis_size(axis), lax.axis_index(axis)
        for step in range(1, size):
            pl.semaphore_signal(
                barrier,
                inc=1,
                device_id={axis: lax.rem(me + step, size)},
                device_id_type=pl.DeviceIdType.MESH,
            )
    pl.semaphore_wait(barrier, sum(lax.axis_size(axis) - 1 for axis in axes))

    def remote(source, target, number, slot, axis, peer):
        return pltpu.make_async_remote_copy(
            src_ref=source,
            dst_ref=target,
            send_sem=send_sems.at[number, slot],
            recv_sem=recv_sems.at[number, slot],
            device_id={axis: peer},
            device_id_type=pl.DeviceIdType.MESH,
        )

    sent, own, relays, landing, planes = [], [], [], [], []

    def pass_on(block, number, slot, axis, peer):
        copy = remote(block, block, number, slot, axis, peer)
        copy.start()
        sent.append(copy)

    def arrived(block, number, slot, axis, origin):
        remote(block, block, number, slot, axis, origin).wait_recv()

    for number, (kind, axis) in enumerate(plan):
        source, target = sources[number], targets[number]
        size, me = lax.axis_size(axis), lax.axis_index(axis)
        mine = source if kind == "gather" else source.at[me]
        own.append(pltpu.make_async_copy(mine, target.at[me], own_sems.at[number]))
        own[-1].start()
        if kind == "gather":
            sibling = me + 1 - 2 * lax.rem(me, 2)
            if size == 8:
                for slot, peer in ((1, flipped(me, 2)), (2, flipped(me, 4))):
                    copy = remote(source, target.at[me], number, slot, axis, peer)
                    copy.start()
                    sent.append(copy)
                copy = remote(source, target.at[me], number, 0, axis, sibling)
                copy.start()
                sent.append(copy)
                planes.append((number, axis, me, sibling))
                continue
            for step in range(1, size // 2):
                copy = remote(
                    source, target.at[me], number, step, axis, lax.rem(me + 2 * step, size)
                )
                copy.start()
                sent.append(copy)
                relays.append((number, axis, step, lax.rem(me + size - 2 * step, size), sibling))
            copy = remote(source, target.at[me], number, 0, axis, sibling)
            copy.start()
            sent.append(copy)
            landing.append(remote(source, target.at[sibling], number, 0, axis, sibling))
            for step in range(1, size // 2):
                origin = lax.rem(sibling + size - 2 * step, size)
                landing.append(
                    remote(source, target.at[origin], number, size // 2 + step, axis, sibling)
                )
        else:
            for step in range(1, size):
                peer = lax.rem(me + step, size)
                copy = remote(source.at[peer], target.at[me], number, step, axis, peer)
                copy.start()
                sent.append(copy)
                origin = lax.rem(me + size - step, size)
                landing.append(
                    remote(source.at[origin], target.at[origin], number, step, axis, origin)
                )
    for number, axis, me, sibling in planes:
        half = sources[number].shape[0] // 2
        near, far = flipped(me, 2), flipped(me, 4)
        for slot, origin, other, start in ((1, near, far, 0), (2, far, near, half)):
            block = targets[number].at[origin]
            arrived(block, number, slot, axis, origin)
            part = targets[number].at[origin, pl.ds(start, half)]
            pass_on(part, number, 2 + slot, axis, other)
            pass_on(block, number, 4 + slot, axis, sibling)
    for number, axis, me, sibling in planes:
        half = sources[number].shape[0] // 2
        near, far = flipped(me, 2), flipped(me, 4)
        across = flipped(near, 4)
        for slot, origin, start in ((3, far, 0), (4, near, half)):
            part = targets[number].at[across, pl.ds(start, half)]
            arrived(part, number, slot, axis, origin)
            pass_on(part, number, 4 + slot, axis, sibling)
    for number, axis, me, sibling in planes:
        half = sources[number].shape[0] // 2
        near, far = flipped(sibling, 2), flipped(sibling, 4)
        across = flipped(near, 4)
        arrived(targets[number].at[sibling], number, 0, axis, sibling)
        arrived(targets[number].at[near], number, 5, axis, sibling)
        arrived(targets[number].at[far], number, 6, axis, sibling)
        for slot, start in ((7, 0), (8, half)):
            part = targets[number].at[across, pl.ds(start, half)]
            arrived(part, number, slot, axis, sibling)
    for number, axis, step, origin, sibling in relays:
        size = lax.axis_size(axis)
        block = targets[number].at[origin]
        remote(sources[number], block, number, step, axis, origin).wait_recv()
        copy = remote(block, block, number, size // 2 + step, axis, sibling)
        copy.start()
        sent.append(copy)
    for copy in landing:
        copy.wait_recv()
    for copy in sent:
        copy.wait_send()
    for copy in own:
        copy.wait()


def exchange(identity, *items):
    plan = tuple((kind, axis) for kind, axis, array in items)
    arrays = [array for kind, axis, array in items]
    shapes = [
        jax.ShapeDtypeStruct(
            ((lax.axis_size(axis),) + array.shape) if kind == "gather" else array.shape,
            array.dtype,
        )
        for kind, axis, array in items
    ]
    slots = max(lax.axis_size(axis) for kind, axis in plan) + 1
    return pl.pallas_call(
        functools.partial(exchange_kernel, plan),
        out_shape=shapes,
        in_specs=[pl.BlockSpec(memory_space=pl.ANY)] * len(arrays),
        out_specs=[pl.BlockSpec(memory_space=pl.ANY)] * len(arrays),
        scratch_shapes=[
            pltpu.SemaphoreType.DMA((len(arrays), slots)),
            pltpu.SemaphoreType.DMA((len(arrays), slots)),
            pltpu.SemaphoreType.DMA((len(arrays),)),
        ],
        compiler_params=pltpu.CompilerParams(collective_id=identity, has_side_effects=True),
    )(*arrays)


def blocks(array, count):
    rows, columns = array.shape
    return array.reshape(rows, count, columns // count).transpose(1, 0, 2)


def merged(array):
    return array.reshape(array.shape[0] * array.shape[1], array.shape[2])


def group_sum(array):
    return jnp.sum(array.astype(jnp.float32), axis=0)


def silu_slope(value):
    sigma = jax.nn.sigmoid(value)
    return sigma * (1.0 + value * (1.0 - sigma))


def norm_rows(value):
    centre = value - jnp.mean(value, axis=-1, keepdims=True)
    inverse = lax.rsqrt(jnp.mean(centre * centre, axis=-1, keepdims=True) + NORM_EPS)
    return (centre * inverse, inverse)


def norm_back(grad, normed, inverse):
    return inverse * (
        grad
        - jnp.mean(grad, axis=-1, keepdims=True)
        - normed * jnp.mean(grad * normed, axis=-1, keepdims=True)
    )


def marks(positions, lengths, targets):
    start = jnp.zeros_like(positions)
    first = jnp.zeros_like(positions)
    end = 0
    for number in range(lengths.shape[1]):
        length = lengths[0, number]
        begin, end = end, end + length
        inside = (positions >= begin) & (positions < end)
        start = jnp.where(inside, begin, start)
        first = jnp.where(inside, end - jnp.minimum(targets[0, number], length - 1), first)
    return start, positions >= first


def seen(query_pos, query_start, key_pos, key_tgt):
    same = (key_pos <= query_pos) & (key_pos >= query_start)
    return same & (jnp.logical_not(key_tgt) | (key_pos == query_pos))


def nt_dot(left, right):
    return lax.dot_general(
        left, right, (((1,), (1,)), ((), ())), preferred_element_type=jnp.float32
    )


def nn_dot(left, right):
    return jnp.dot(left, right, preferred_element_type=jnp.float32)


def store_blocks(target, value):
    width = target.shape[2]
    for number in range(target.shape[0]):
        target[number] = value[:, number * width : (number + 1) * width]


def head_cols(ref, column):
    part = ref[:, :, column : column + DH]
    return part.reshape(part.shape[0] * part.shape[1], DH)


def opening_kernel(x_ref, w_in_ref, normed_ref, pre_ref, gate_ref, rest_ref):
    normed, inverse = norm_rows(x_ref[...].astype(jnp.float32))
    normed_b = normed.astype(jnp.bfloat16)
    store_blocks(normed_ref, normed_b)
    width = gate_ref.shape[1]
    for number in range(4):
        columns = slice(number * width, (number + 1) * width)
        pre = nn_dot(normed_b, w_in_ref[:, columns])
        pre_ref[:, columns] = pre
        hidden_b = jax.nn.silu(pre).astype(jnp.bfloat16)
        if number == 0:
            gate_ref[...] = hidden_b
        else:
            rest_ref[:, (number - 1) * width : number * width] = hidden_b


def middle_kernel(
    divisor,
    lengths,
    targets,
    own_start,
    moved_ref,
    own_ref,
    gate_ref,
    pre_ref,
    x_ref,
    grad_ref,
    score_ref,
    head_score_ref,
    w_out_ref,
    w_score_ref,
    d_att_ref,
    d_total_ref,
    d_total_b_ref,
    d_mid_ref,
    head_ref,
    gated_ref,
    out_ref,
    d_pre_ref,
    attended_ref,
):
    rows, width = gate_ref.shape
    total = moved_ref.shape[0] * rows
    query_pos = own_start[0] + lax.broadcasted_iota(jnp.int32, (rows, 1), 0)
    key_pos = lax.broadcasted_iota(jnp.int32, (1, total), 1)
    query_start, query_tgt = marks(query_pos, lengths, targets)
    unused, key_tgt = marks(key_pos, lengths, targets)
    mask = seen(query_pos, query_start, key_pos, key_tgt)
    for head in range(HEADS):
        column = head * DH
        query = own_ref[:, width + column : width + column + DH]
        raw = nt_dot(query, head_cols(moved_ref, 2 * width + column)) * DH ** (-0.5)
        attn_b = jnp.where(mask, jax.nn.silu(raw) / divisor, 0.0).astype(jnp.bfloat16)
        attended_ref[:, column : column + DH] = nn_dot(attn_b, head_cols(moved_ref, column))
    onorm, att_inverse = norm_rows(attended_ref[...])
    gate_f = gate_ref[...].astype(jnp.float32)
    gated_b = (onorm * gate_f).astype(jnp.bfloat16)
    store_blocks(gated_ref, gated_b)
    output = x_ref[...].astype(jnp.float32) + nn_dot(gated_b, w_out_ref[...])
    out_b = output.astype(jnp.bfloat16)
    store_blocks(out_ref, out_b)
    mid_act = nn_dot(out_b, w_score_ref[...])
    weight_c = score_ref[...] * query_tgt.astype(jnp.float32)
    head_part = jnp.sum(weight_c * jax.nn.silu(mid_act), axis=0, keepdims=True)
    head_ref[...] = jnp.broadcast_to(head_part, head_ref.shape)
    d_mid_b = (weight_c * head_score_ref[...] * silu_slope(mid_act)).astype(jnp.bfloat16)
    d_mid_ref[...] = d_mid_b
    d_total = grad_ref[...].astype(jnp.float32) + nt_dot(d_mid_b, w_score_ref[...])
    d_total_ref[...] = d_total
    d_total_b = d_total.astype(jnp.bfloat16)
    d_total_b_ref[...] = d_total_b
    d_gated = nt_dot(d_total_b, w_out_ref[...])
    d_pre_ref[...] = (d_gated * onorm * silu_slope(pre_ref[:, 0:width])).astype(jnp.bfloat16)
    d_att_ref[...] = norm_back(d_gated * gate_f, onorm, att_inverse).astype(jnp.bfloat16)


def closing_kernel(
    divisor,
    lengths,
    targets,
    own_start,
    moved_ref,
    grad_all_ref,
    own_ref,
    own_grad_ref,
    pre_ref,
    d_pre_gate_ref,
    x_ref,
    d_total_ref,
    w_in_ref,
    d_pre_ref,
    d_x_ref,
):
    rows, width = own_grad_ref.shape
    total = moved_ref.shape[0] * rows
    own_col = own_start[0] + lax.broadcasted_iota(jnp.int32, (rows, 1), 0)
    all_row = lax.broadcasted_iota(jnp.int32, (1, total), 1)
    own_first, own_tgt = marks(own_col, lengths, targets)
    all_first, all_tgt = marks(all_row, lengths, targets)
    mask = seen(own_col, own_first, all_row, all_tgt)
    key_mask = seen(all_row, all_first, own_col, own_tgt)
    scale = DH ** (-0.5)

    def store(kind, column, value):
        columns = slice(kind * width + column, kind * width + column + DH)
        slope = silu_slope(pre_ref[:, columns])
        d_pre_ref[:, columns] = (value * slope).astype(jnp.bfloat16)

    d_pre_ref[:, 0:width] = d_pre_gate_ref[...]
    for head in range(HEADS):
        column = head * DH
        value_own = own_ref[:, column : column + DH]
        query_own = own_ref[:, width + column : width + column + DH]
        key_own = own_ref[:, 2 * width + column : 2 * width + column + DH]
        grad_own = own_grad_ref[:, column : column + DH]
        value_all = head_cols(moved_ref, column)
        query_all = head_cols(moved_ref, width + column)
        key_all = head_cols(moved_ref, 2 * width + column)
        grad_all = head_cols(grad_all_ref, column)
        raw = nt_dot(query_own, key_all) * scale
        factor = jnp.where(mask, silu_slope(raw) * scale / divisor, 0.0)
        d_raw_b = (nt_dot(grad_own, value_all) * factor).astype(jnp.bfloat16)
        store(2, column, nn_dot(d_raw_b, key_all))
        raw = nt_dot(key_own, query_all) * scale
        sigma = jax.nn.sigmoid(raw)
        attn_b = jnp.where(key_mask, raw * sigma / divisor, 0.0).astype(jnp.bfloat16)
        slope = sigma * (1.0 + raw * (1.0 - sigma))
        factor = jnp.where(key_mask, slope * scale / divisor, 0.0)
        d_raw_b = (nt_dot(value_own, grad_all) * factor).astype(jnp.bfloat16)
        store(3, column, nn_dot(d_raw_b, query_all))
        store(1, column, nn_dot(attn_b, grad_all))
    normed, inverse = norm_rows(x_ref[...].astype(jnp.float32))
    d_normed = nt_dot(d_pre_ref[...], w_in_ref[...])
    d_x = d_total_ref[...] + norm_back(d_normed, normed, inverse)
    d_x_ref[...] = d_x.astype(jnp.bfloat16)


def local_call(kernel, scalars, arrays, outs, scratch=()):
    return pl.pallas_call(
        kernel,
        out_shape=[jax.ShapeDtypeStruct(shape, kind) for shape, kind in outs],
        in_specs=[pl.BlockSpec(memory_space=pltpu.SMEM)] * len(scalars)
        + [pl.BlockSpec(memory_space=pltpu.VMEM)] * len(arrays),
        out_specs=[pl.BlockSpec(memory_space=pltpu.VMEM)] * len(outs),
        scratch_shapes=list(scratch),
        compiler_params=pltpu.CompilerParams(vmem_limit_bytes=56 * 1024 * 1024),
    )(*scalars, *arrays)


def on_device(x_rows, lengths, targets, w_in, w_out, w_score, head_score, grad_out, grad_score):
    rows, features = x_rows.shape[1:]
    seq_count = lax.axis_size("seq")
    group_count = lax.axis_size("dp")
    total = rows * seq_count
    width = w_out.shape[0]
    middle = head_score.shape[0]
    divisor = float(total // 2)
    half, full = jnp.bfloat16, jnp.float32
    own_start = (lax.axis_index("seq") * rows).astype(jnp.int32)[None]
    scalars = (lengths, targets, own_start)
    normed_blocks, pre_act, gate_b, own_b = local_call(
        opening_kernel,
        (),
        (x_rows[0], w_in),
        (
            ((seq_count, rows, features // seq_count), half),
            ((rows, 4 * width), full),
            ((rows, width), half),
            ((rows, 3 * width), half),
        ),
    )
    moved, normed_cols = exchange(
        1, ("gather", "seq", own_b), ("swap", "seq", normed_blocks)
    )
    d_att_b, d_total, d_total_b, d_mid_b, head_part, gated_blocks, out_blocks, d_pre_gate = (
        local_call(
            functools.partial(middle_kernel, divisor),
            scalars,
            (
                moved,
                own_b,
                gate_b,
                pre_act,
                x_rows[0],
                grad_out[0],
                grad_score[0][:, None],
                head_score[None, :],
                w_out,
                w_score,
            ),
            (
                ((rows, width), half),
                ((rows, features), full),
                ((rows, features), half),
                ((rows, middle), half),
                ((16, middle), full),
                ((seq_count, rows, width // seq_count), half),
                ((seq_count, rows, features // seq_count), half),
                ((rows, width), half),
            ),
            (pltpu.VMEM((rows, width), full),),
        )
    )
    grad_all, total_all, mid_all, head_all, gated_cols, out_cols = exchange(
        2,
        ("gather", "seq", d_att_b),
        ("gather", "seq", d_total_b),
        ("gather", "seq", d_mid_b),
        ("gather", "seq", head_part),
        ("swap", "seq", gated_blocks),
        ("swap", "seq", out_blocks),
    )
    out_part = nn_dot(merged(gated_cols).T, merged(total_all))
    score_part = nn_dot(merged(out_cols).T, merged(mid_all))
    head_group = jnp.sum(head_all, axis=0)
    d_pre_b, d_x = local_call(
        functools.partial(closing_kernel, divisor),
        scalars,
        (moved, grad_all, own_b, d_att_b, pre_act, d_pre_gate, x_rows[0], d_total, w_in),
        (((rows, 4 * width), half), ((rows, features), half)),
    )
    pre_all, out_parts, score_parts, head_parts = exchange(
        3,
        ("gather", "seq", d_pre_b),
        ("swap", "dp", blocks(out_part.astype(half), group_count)),
        ("swap", "dp", blocks(score_part.astype(half), group_count)),
        ("swap", "dp", jnp.broadcast_to(head_group, (group_count,) + head_group.shape)),
    )
    in_part = nn_dot(merged(normed_cols).T, merged(pre_all))
    (in_parts,) = exchange(4, ("swap", "dp", blocks(in_part.astype(half), group_count)))
    return (
        d_x[None],
        group_sum(in_parts),
        group_sum(out_parts),
        group_sum(score_parts),
        group_sum(head_parts)[0],
    )


def solution(mesh):
    placed = (
        P("dp", "seq", None),
        P("dp", None),
        P("dp", None),
        P(),
        P(),
        P(),
        P(),
        P("dp", "seq", None),
        P("dp", "seq"),
    )
    return jax.shard_map(
        on_device,
        mesh=mesh,
        in_specs=placed,
        out_specs=(P("dp", "seq", None), P("seq", "dp"), P("seq", "dp"), P("seq", "dp"), P()),
        check_vma=False,
    )
```

```python
import functools

import jax
import jax.numpy as jnp
from jax import lax
from jax.experimental import pallas as pl
from jax.experimental.pallas import tpu as pltpu
from jax.sharding import PartitionSpec as P

HEADS = 4
DH = 128


NORM_EPS = 1e-05


def flipped(index, bit):
    return index + bit - 2 * bit * lax.rem(index // bit, 2)


def exchange_kernel(plan, *refs):
    count = len(plan)
    sources, targets = refs[:count], refs[count : 2 * count]
    send_sems, recv_sems, own_sems = refs[2 * count :]
    axes = sorted({axis for kind, axis in plan})
    barrier = pltpu.get_barrier_semaphore()
    for axis in axes:
        size, me = lax.axis_size(axis), lax.axis_index(axis)
        for step in range(1, size):
            pl.semaphore_signal(
                barrier,
                inc=1,
                device_id={axis: lax.rem(me + step, size)},
                device_id_type=pl.DeviceIdType.MESH,
            )
    pl.semaphore_wait(barrier, sum(lax.axis_size(axis) - 1 for axis in axes))

    def remote(source, target, number, slot, axis, peer):
        return pltpu.make_async_remote_copy(
            src_ref=source,
            dst_ref=target,
            send_sem=send_sems.at[number, slot],
            recv_sem=recv_sems.at[number, slot],
            device_id={axis: peer},
            device_id_type=pl.DeviceIdType.MESH,
        )

    sent, own, relays, landing, planes = [], [], [], [], []

    def pass_on(block, number, slot, axis, peer):
        copy = remote(block, block, number, slot, axis, peer)
        copy.start()
        sent.append(copy)

    def arrived(block, number, slot, axis, origin):
        remote(block, block, number, slot, axis, origin).wait_recv()

    for number, (kind, axis) in enumerate(plan):
        source, target = sources[number], targets[number]
        size, me = lax.axis_size(axis), lax.axis_index(axis)
        mine = source if kind == "gather" else source.at[me]
        own.append(pltpu.make_async_copy(mine, target.at[me], own_sems.at[number]))
        own[-1].start()
        if kind == "gather":
            sibling = me + 1 - 2 * lax.rem(me, 2)
            if size == 8:
                for slot, peer in ((1, flipped(me, 2)), (2, flipped(me, 4))):
                    copy = remote(source, target.at[me], number, slot, axis, peer)
                    copy.start()
                    sent.append(copy)
                copy = remote(source, target.at[me], number, 0, axis, sibling)
                copy.start()
                sent.append(copy)
                planes.append((number, axis, me, sibling))
                continue
            for step in range(1, size // 2):
                copy = remote(
                    source, target.at[me], number, step, axis, lax.rem(me + 2 * step, size)
                )
                copy.start()
                sent.append(copy)
                relays.append((number, axis, step, lax.rem(me + size - 2 * step, size), sibling))
            copy = remote(source, target.at[me], number, 0, axis, sibling)
            copy.start()
            sent.append(copy)
            landing.append(remote(source, target.at[sibling], number, 0, axis, sibling))
            for step in range(1, size // 2):
                origin = lax.rem(sibling + size - 2 * step, size)
                landing.append(
                    remote(source, target.at[origin], number, size // 2 + step, axis, sibling)
                )
        else:
            for step in range(1, size):
                peer = lax.rem(me + step, size)
                copy = remote(source.at[peer], target.at[me], number, step, axis, peer)
                copy.start()
                sent.append(copy)
                origin = lax.rem(me + size - step, size)
                landing.append(
                    remote(source.at[origin], target.at[origin], number, step, axis, origin)
                )
    for number, axis, me, sibling in planes:
        half = sources[number].shape[0] // 2
        near, far = flipped(me, 2), flipped(me, 4)
        for slot, origin, other, start in ((1, near, far, 0), (2, far, near, half)):
            block = targets[number].at[origin]
            arrived(block, number, slot, axis, origin)
            part = targets[number].at[origin, pl.ds(start, half)]
            pass_on(part, number, 2 + slot, axis, other)
            pass_on(block, number, 4 + slot, axis, sibling)
    for number, axis, me, sibling in planes:
        half = sources[number].shape[0] // 2
        near, far = flipped(me, 2), flipped(me, 4)
        across = flipped(near, 4)
        for slot, origin, start in ((3, far, 0), (4, near, half)):
            part = targets[number].at[across, pl.ds(start, half)]
            arrived(part, number, slot, axis, origin)
            pass_on(part, number, 4 + slot, axis, sibling)
    for number, axis, me, sibling in planes:
        half = sources[number].shape[0] // 2
        near, far = flipped(sibling, 2), flipped(sibling, 4)
        across = flipped(near, 4)
        arrived(targets[number].at[sibling], number, 0, axis, sibling)
        arrived(targets[number].at[near], number, 5, axis, sibling)
        arrived(targets[number].at[far], number, 6, axis, sibling)
        for slot, start in ((7, 0), (8, half)):
            part = targets[number].at[across, pl.ds(start, half)]
            arrived(part, number, slot, axis, sibling)
    for number, axis, step, origin, sibling in relays:
        size = lax.axis_size(axis)
        block = targets[number].at[origin]
        remote(sources[number], block, number, step, axis, origin).wait_recv()
        copy = remote(block, block, number, size // 2 + step, axis, sibling)
        copy.start()
        sent.append(copy)
    for copy in landing:
        copy.wait_recv()
    for copy in sent:
        copy.wait_send()
    for copy in own:
        copy.wait()


def exchange(identity, *items):
    plan = tuple((kind, axis) for kind, axis, array in items)
    arrays = [array for kind, axis, array in items]
    shapes = [
        jax.ShapeDtypeStruct(
            ((lax.axis_size(axis),) + array.shape) if kind == "gather" else array.shape,
            array.dtype,
        )
        for kind, axis, array in items
    ]
    slots = max(lax.axis_size(axis) for kind, axis in plan) + 1
    return pl.pallas_call(
        functools.partial(exchange_kernel, plan),
        out_shape=shapes,
        in_specs=[pl.BlockSpec(memory_space=pl.ANY)] * len(arrays),
        out_specs=[pl.BlockSpec(memory_space=pl.ANY)] * len(arrays),
        scratch_shapes=[
            pltpu.SemaphoreType.DMA((len(arrays), slots)),
            pltpu.SemaphoreType.DMA((len(arrays), slots)),
            pltpu.SemaphoreType.DMA((len(arrays),)),
        ],
        compiler_params=pltpu.CompilerParams(collective_id=identity, has_side_effects=True),
    )(*arrays)


def blocks(array, count):
    rows, columns = array.shape
    return array.reshape(rows, count, columns // count).transpose(1, 0, 2)


def merged(array):
    return array.reshape(array.shape[0] * array.shape[1], array.shape[2])


def group_sum(array):
    return jnp.sum(array.astype(jnp.float32), axis=0)


def silu_slope(value):
    sigma = jax.nn.sigmoid(value)
    return sigma * (1.0 + value * (1.0 - sigma))


def norm_rows(value):
    centre = value - jnp.mean(value, axis=-1, keepdims=True)
    inverse = lax.rsqrt(jnp.mean(centre * centre, axis=-1, keepdims=True) + NORM_EPS)
    return (centre * inverse, inverse)


def norm_back(grad, normed, inverse):
    return inverse * (
        grad
        - jnp.mean(grad, axis=-1, keepdims=True)
        - normed * jnp.mean(grad * normed, axis=-1, keepdims=True)
    )


def marks(positions, lengths, targets):
    start = jnp.zeros_like(positions)
    first = jnp.zeros_like(positions)
    end = 0
    for number in range(lengths.shape[1]):
        length = lengths[0, number]
        begin, end = end, end + length
        inside = (positions >= begin) & (positions < end)
        start = jnp.where(inside, begin, start)
        first = jnp.where(inside, end - jnp.minimum(targets[0, number], length - 1), first)
    return start, positions >= first


def seen(query_pos, query_start, key_pos, key_tgt):
    same = (key_pos <= query_pos) & (key_pos >= query_start)
    return same & (jnp.logical_not(key_tgt) | (key_pos == query_pos))


def nt_dot(left, right):
    return lax.dot_general(
        left, right, (((1,), (1,)), ((), ())), preferred_element_type=jnp.float32
    )


def nn_dot(left, right):
    return jnp.dot(left, right, preferred_element_type=jnp.float32)


def store_blocks(target, value):
    width = target.shape[2]
    for number in range(target.shape[0]):
        target[number] = value[:, number * width : (number + 1) * width]


def head_cols(ref, column):
    part = ref[:, :, column : column + DH]
    return part.reshape(part.shape[0] * part.shape[1], DH)


def opening_kernel(x_ref, w_in_ref, normed_ref, pre_ref, gate_ref, rest_ref):
    normed, inverse = norm_rows(x_ref[...].astype(jnp.float32))
    normed_b = normed.astype(jnp.bfloat16)
    store_blocks(normed_ref, normed_b)
    width = gate_ref.shape[1]
    for number in range(4):
        columns = slice(number * width, (number + 1) * width)
        pre = nn_dot(normed_b, w_in_ref[:, columns])
        pre_ref[:, columns] = pre
        hidden_b = jax.nn.silu(pre).astype(jnp.bfloat16)
        if number == 0:
            gate_ref[...] = hidden_b
        else:
            rest_ref[:, (number - 1) * width : number * width] = hidden_b


def middle_kernel(
    divisor,
    lengths,
    targets,
    own_start,
    moved_ref,
    own_ref,
    gate_ref,
    pre_ref,
    x_ref,
    grad_ref,
    score_ref,
    head_score_ref,
    w_out_ref,
    w_score_ref,
    d_att_ref,
    d_total_ref,
    d_total_b_ref,
    d_mid_ref,
    head_ref,
    gated_ref,
    out_ref,
    d_pre_ref,
    attended_ref,
):
    rows, width = gate_ref.shape
    total = moved_ref.shape[0] * rows
    query_pos = own_start[0] + lax.broadcasted_iota(jnp.int32, (rows, 1), 0)
    key_pos = lax.broadcasted_iota(jnp.int32, (1, total), 1)
    query_start, query_tgt = marks(query_pos, lengths, targets)
    unused, key_tgt = marks(key_pos, lengths, targets)
    mask = seen(query_pos, query_start, key_pos, key_tgt)
    for head in range(HEADS):
        column = head * DH
        query = own_ref[:, width + column : width + column + DH]
        raw = nt_dot(query, head_cols(moved_ref, 2 * width + column)) * DH ** (-0.5)
        attn_b = jnp.where(mask, jax.nn.silu(raw) / divisor, 0.0).astype(jnp.bfloat16)
        attended_ref[:, column : column + DH] = nn_dot(attn_b, head_cols(moved_ref, column))
    onorm, att_inverse = norm_rows(attended_ref[...])
    gate_f = gate_ref[...].astype(jnp.float32)
    gated_b = (onorm * gate_f).astype(jnp.bfloat16)
    store_blocks(gated_ref, gated_b)
    output = x_ref[...].astype(jnp.float32) + nn_dot(gated_b, w_out_ref[...])
    out_b = output.astype(jnp.bfloat16)
    store_blocks(out_ref, out_b)
    mid_act = nn_dot(out_b, w_score_ref[...])
    diagonal = lax.broadcasted_iota(jnp.int32, (rows, rows), 0) == lax.broadcasted_iota(
        jnp.int32, (rows, rows), 1
    )
    score_col = jnp.sum(jnp.where(diagonal, score_ref[...], 0.0), axis=1, keepdims=True)
    weight_c = score_col * query_tgt.astype(jnp.float32)
    head_part = jnp.sum(weight_c * jax.nn.silu(mid_act), axis=0, keepdims=True)
    head_ref[...] = jnp.broadcast_to(head_part, head_ref.shape)
    d_mid_b = (weight_c * head_score_ref[...] * silu_slope(mid_act)).astype(jnp.bfloat16)
    d_mid_ref[...] = d_mid_b
    d_total = grad_ref[...].astype(jnp.float32) + nt_dot(d_mid_b, w_score_ref[...])
    d_total_ref[...] = d_total
    d_total_b = d_total.astype(jnp.bfloat16)
    d_total_b_ref[...] = d_total_b
    d_gated = nt_dot(d_total_b, w_out_ref[...])
    d_pre_ref[...] = (d_gated * onorm * silu_slope(pre_ref[:, 0:width])).astype(jnp.bfloat16)
    d_att_ref[...] = norm_back(d_gated * gate_f, onorm, att_inverse).astype(jnp.bfloat16)


def closing_kernel(
    divisor,
    lengths,
    targets,
    own_start,
    moved_ref,
    grad_all_ref,
    own_ref,
    own_grad_ref,
    pre_ref,
    d_pre_gate_ref,
    x_ref,
    d_total_ref,
    w_in_ref,
    d_pre_ref,
    d_x_ref,
):
    rows, width = own_grad_ref.shape
    total = moved_ref.shape[0] * rows
    own_col = own_start[0] + lax.broadcasted_iota(jnp.int32, (rows, 1), 0)
    all_row = lax.broadcasted_iota(jnp.int32, (1, total), 1)
    own_first, own_tgt = marks(own_col, lengths, targets)
    all_first, all_tgt = marks(all_row, lengths, targets)
    mask = seen(own_col, own_first, all_row, all_tgt)
    key_mask = seen(all_row, all_first, own_col, own_tgt)
    scale = DH ** (-0.5)

    def store(kind, column, value):
        columns = slice(kind * width + column, kind * width + column + DH)
        slope = silu_slope(pre_ref[:, columns])
        d_pre_ref[:, columns] = (value * slope).astype(jnp.bfloat16)

    d_pre_ref[:, 0:width] = d_pre_gate_ref[...]
    for head in range(HEADS):
        column = head * DH
        value_own = own_ref[:, column : column + DH]
        query_own = own_ref[:, width + column : width + column + DH]
        key_own = own_ref[:, 2 * width + column : 2 * width + column + DH]
        grad_own = own_grad_ref[:, column : column + DH]
        value_all = head_cols(moved_ref, column)
        query_all = head_cols(moved_ref, width + column)
        key_all = head_cols(moved_ref, 2 * width + column)
        grad_all = head_cols(grad_all_ref, column)
        raw = nt_dot(query_own, key_all) * scale
        factor = jnp.where(mask, silu_slope(raw) * scale / divisor, 0.0)
        d_raw_b = (nt_dot(grad_own, value_all) * factor).astype(jnp.bfloat16)
        store(2, column, nn_dot(d_raw_b, key_all))
        raw = nt_dot(key_own, query_all) * scale
        sigma = jax.nn.sigmoid(raw)
        attn_b = jnp.where(key_mask, raw * sigma / divisor, 0.0).astype(jnp.bfloat16)
        slope = sigma * (1.0 + raw * (1.0 - sigma))
        factor = jnp.where(key_mask, slope * scale / divisor, 0.0)
        d_raw_b = (nt_dot(value_own, grad_all) * factor).astype(jnp.bfloat16)
        store(3, column, nn_dot(d_raw_b, query_all))
        store(1, column, nn_dot(attn_b, grad_all))
    normed, inverse = norm_rows(x_ref[...].astype(jnp.float32))
    d_normed = nt_dot(d_pre_ref[...], w_in_ref[...])
    d_x = d_total_ref[...] + norm_back(d_normed, normed, inverse)
    d_x_ref[...] = d_x.astype(jnp.bfloat16)


def local_call(kernel, scalars, arrays, outs, scratch=()):
    return pl.pallas_call(
        kernel,
        out_shape=[jax.ShapeDtypeStruct(shape, kind) for shape, kind in outs],
        in_specs=[pl.BlockSpec(memory_space=pltpu.SMEM)] * len(scalars)
        + [pl.BlockSpec(memory_space=pltpu.VMEM)] * len(arrays),
        out_specs=[pl.BlockSpec(memory_space=pltpu.VMEM)] * len(outs),
        scratch_shapes=list(scratch),
        compiler_params=pltpu.CompilerParams(vmem_limit_bytes=56 * 1024 * 1024),
    )(*scalars, *arrays)


def on_device(x_rows, lengths, targets, w_in, w_out, w_score, head_score, grad_out, grad_score):
    rows, features = x_rows.shape[1:]
    seq_count = lax.axis_size("seq")
    group_count = lax.axis_size("dp")
    total = rows * seq_count
    width = w_out.shape[0]
    middle = head_score.shape[0]
    divisor = float(total // 2)
    half, full = jnp.bfloat16, jnp.float32
    own_start = (lax.axis_index("seq") * rows).astype(jnp.int32)[None]
    scalars = (lengths, targets, own_start)
    normed_blocks, pre_act, gate_b, own_b = local_call(
        opening_kernel,
        (),
        (x_rows[0], w_in),
        (
            ((seq_count, rows, features // seq_count), half),
            ((rows, 4 * width), full),
            ((rows, width), half),
            ((rows, 3 * width), half),
        ),
    )
    moved, normed_cols = exchange(
        1, ("gather", "seq", own_b), ("swap", "seq", normed_blocks)
    )
    d_att_b, d_total, d_total_b, d_mid_b, head_part, gated_blocks, out_blocks, d_pre_gate = (
        local_call(
            functools.partial(middle_kernel, divisor),
            scalars,
            (
                moved,
                own_b,
                gate_b,
                pre_act,
                x_rows[0],
                grad_out[0],
                grad_score,
                head_score[None, :],
                w_out,
                w_score,
            ),
            (
                ((rows, width), half),
                ((rows, features), full),
                ((rows, features), half),
                ((rows, middle), half),
                ((16, middle), full),
                ((seq_count, rows, width // seq_count), half),
                ((seq_count, rows, features // seq_count), half),
                ((rows, width), half),
            ),
            (pltpu.VMEM((rows, width), full),),
        )
    )
    grad_all, total_all, mid_all, head_all, gated_cols, out_cols = exchange(
        2,
        ("gather", "seq", d_att_b),
        ("gather", "seq", d_total_b),
        ("gather", "seq", d_mid_b),
        ("gather", "seq", head_part),
        ("swap", "seq", gated_blocks),
        ("swap", "seq", out_blocks),
    )
    out_part = nn_dot(merged(gated_cols).T, merged(total_all))
    score_part = nn_dot(merged(out_cols).T, merged(mid_all))
    head_group = jnp.sum(head_all, axis=0)
    d_pre_b, d_x = local_call(
        functools.partial(closing_kernel, divisor),
        scalars,
        (moved, grad_all, own_b, d_att_b, pre_act, d_pre_gate, x_rows[0], d_total, w_in),
        (((rows, 4 * width), half), ((rows, features), half)),
    )
    pre_all, out_parts, score_parts, head_parts = exchange(
        3,
        ("gather", "seq", d_pre_b),
        ("swap", "dp", blocks(out_part.astype(half), group_count)),
        ("swap", "dp", blocks(score_part.astype(half), group_count)),
        ("swap", "dp", jnp.broadcast_to(head_group, (group_count,) + head_group.shape)),
    )
    in_part = nn_dot(merged(normed_cols).T, merged(pre_all))
    (in_parts,) = exchange(4, ("swap", "dp", blocks(in_part.astype(half), group_count)))
    return (
        d_x[None],
        group_sum(in_parts),
        group_sum(out_parts),
        group_sum(score_parts),
        group_sum(head_parts)[0],
    )


def solution(mesh):
    placed = (
        P("dp", "seq", None),
        P("dp", None),
        P("dp", None),
        P(),
        P(),
        P(),
        P(),
        P("dp", "seq", None),
        P("dp", "seq"),
    )
    return jax.shard_map(
        on_device,
        mesh=mesh,
        in_specs=placed,
        out_specs=(P("dp", "seq", None), P("seq", "dp"), P("seq", "dp"), P("seq", "dp"), P()),
        check_vma=False,
    )
```
